32 devices in a mesh: replica: 2 (over y), rows: 4 (over x, core), tensor: 4 (over z).
Axes of the slice: x: 2, y: 2, z: 4, core: 2. Of those that a mesh axis runs over, the one named last changes fastest.
Arguments:
- gate_in: bfloat16 [512, 16384], P(('replica', 'rows'), 'tensor'), parts along dimension 0, may hold values from -6 to 6
- up_in: bfloat16 [512, 16384], P(('replica', 'rows'), 'tensor'), parts along dimension 0, may hold values from -6 to 6
- down_weight: bfloat16 [16384, 8192], P('tensor', 'rows'), may hold values from -0.046875 to 0.046875
- delta_tiles: bfloat16 [4, 128, 6, 128, 128], P('rows', 'tensor'), may hold values from -0.15625 to 0.15625
- delta_cols: int32 [4, 128, 6], P('rows', 'tensor'), may hold values from 0 to 63, as said below
- tenant_of_row: int32 [512, 1], P(('replica', 'rows')), parts along dimension 0, may hold values from 0 to 3; in each aligned block of 64 rows (0 to 63, 64 to 127, ...) at most 24 rows name the same one
Outputs:
- mixed: bfloat16 [512, 8192], P(('replica', 'rows'), 'tensor'), parts along dimension 0
The draws below stay inside these ranges and needn't reach their ends.
There are 2 independent parts, one for each index of `replica`. The reference program is written for one: setup_inputs(seed, part) draws one part's arguments, and reference() takes and returns one part's arrays. A program takes and returns all parts, laid end to end along the dimension named above; an argument that names none is the same for every part. Nothing has to cross between parts.
Inputs may be any that keep to these rules, and one draw needn't show every extreme that they name: `tenant_of_row`: tenant k's delta is held by row group k. Within the rows of one row group no tenant has more than 24 rows, and in every draw some tenant has exactly 24 in some group. `delta_cols`: the 6 tiles of one row of tiles of a tenant's delta have distinct column blocks.
All inputs are finite; a program needn't handle non-finite values.
Results may differ from the reference program's by a relative error of at most 0.009.
Values may be sent and summed in bfloat16 or wider, within the bound.
No kernel may reach another device: no remote copies, remote signals or barrier semaphores. Data moves between devices by JAX's collectives and lax.ppermute only.
A program may use at most 128 MiB of HBM per device.

```python
import math
import jax
import jax.numpy as jnp
import numpy as np
from jax import lax

D = 8192
FF = 16384
TPR = 6
TOK_GRP = 64
TENANTS = 4
CAP = 24
TOKENS = 256
N_ROWS = 4
N_TENSOR = 4


def draw_delta_cols(key, part):
    key = jax.random.fold_in(key, 7)
    nrow = TENANTS * (FF // 128)
    ncol = D // 128
    scores = jax.random.randint(key, (nrow, ncol), 0, 1 << 20) * ncol + jnp.arange(ncol, dtype=jnp.int32)[None, :]
    order = jnp.argsort(scores, axis=1)
    return order[:, :TPR].astype(jnp.int32).reshape(TENANTS, FF // 128, TPR)


def shard_levels(own_key, shape, cuts, low, high):
    level, own = 1.0, jax.random.fold_in(own_key, 6)
    for dim, blocks in cuts:
        heights = jnp.exp(jax.random.uniform(jax.random.fold_in(own, dim), (blocks,), jnp.float32, low / len(cuts), high / len(cuts)))
        level = level * jnp.repeat(heights, shape[dim] // blocks).reshape([-1 if axis == dim else 1 for axis in range(len(shape))])
    return level


def assign_block(key, own, number, rows, count, top, most, skew):
    order = jax.random.permutation(key, count)
    crowded, common = portions_of(count, rows * top, most, skew, True), portions_of(count, rows * top, most, skew, False)
    places = jnp.arange(count)

    def named(lengths, turn):
        used = int((lengths > 0).sum())
        fixed = max(1, used // 4)
        passed = fixed + (places - fixed + turn * (used - fixed)) % max(1, count - fixed)
        return jnp.zeros((count,), jnp.int32).at[order[jnp.where(places < fixed, places, passed)]].set(jnp.asarray(lengths, jnp.int32))

    lengths = jnp.where(number % 4 == 0, named(crowded, number // 4), named(common, number - number // 4 - 1))
    mixed = jax.random.permutation(jax.random.fold_in(own, 3), count)
    donor, taker = mixed[0:count // 2 * 2:2], mixed[1:count // 2 * 2:2]
    margin = jnp.minimum(lengths[donor] - 1, most - lengths[taker]) // 2
    margin = jnp.where((donor == order[0]) | (taker == order[0]) | (lengths[taker] == 0), 0, jnp.maximum(margin, 0))
    passed = jax.random.randint(jax.random.fold_in(own, 4), (count // 2,), 0, 1 << 20) % (margin + 1)
    lengths = lengths.at[donor].add(-passed).at[taker].add(passed)
    members = jnp.searchsorted(jnp.cumsum(lengths), jnp.arange(rows * top), side="right").astype(jnp.int32)
    table = members.reshape(top, rows).T
    table = table[jax.random.permutation(jax.random.fold_in(own, 1), rows)]
    turn = jax.random.randint(jax.random.fold_in(own, 2), (rows, 1), 0, top)
    return jnp.take_along_axis(table, (jnp.arange(top)[None, :] + turn) % top, axis=1)


def portions_of(count, total, most, lean, full):
    weights = [(1 << 20) // math.isqrt(standing ** lean) + 1 for standing in range(1, count + 1)]
    largest = most if full else min(most, max(-(-total // count), total * weights[0] // sum(weights)))
    least = 1 if total - largest >= count - 1 else 0
    counts, rest = [largest] + [least] * (count - 1), total - largest - least * (count - 1)
    while rest > 0:
        candidates = [i for i in range(1, count) if counts[i] < largest] or [i for i in range(1, count) if counts[i] < most]
        mass, remaining = sum([weights[i] for i in candidates]), rest
        for i in candidates:
            more = min(most - counts[i], max(1, remaining * weights[i] // mass), rest)
            counts[i] = counts[i] + more
            rest = rest - more
    return np.array(counts)


def bell_draw(stream_key, dims, scale, limit, cuts=(), kind=jnp.bfloat16):
    factor_of = shard_levels(stream_key, dims, cuts, -0.22, 0.18) if cuts else 1.0
    drawn = jax.random.normal(stream_key, dims, jnp.float32) * scale * factor_of
    return jnp.minimum(jnp.maximum(drawn, -limit), limit).astype(kind)


def setup_inputs(seed: int = 0, part: int = 0) -> dict:
    arg_keys = jax.random.split(jax.random.key(seed), 7)
    part_keys = jax.random.split(jax.random.fold_in(arg_keys[6], part), 7)
    gate_in = bell_draw(part_keys[0], (TOKENS, FF), 1.0, 6.0, ((0, 4), (1, 4)))
    up_in = bell_draw(part_keys[1], (TOKENS, FF), 1.0, 6.0, ((0, 4), (1, 4)))
    down_weight = bell_draw(arg_keys[2], (FF, D), FF ** -0.5, 0.046875, ((0, 4), (1, 4)))
    delta_tiles = bell_draw(arg_keys[3], (TENANTS, FF // 128, TPR, 128, 128), (FF * TPR * 128 // D) ** -0.5, 0.15625, ((0, 4), (1, 4)))
    delta_cols = draw_delta_cols(jax.random.fold_in(arg_keys[6], 71), part)
    tenant_of_row_keys = jax.random.split(jax.random.fold_in(part_keys[5], 1), TOKENS // TOK_GRP)
    tenant_of_row_turns = jax.random.permutation(jax.random.fold_in(part_keys[5], 3), TOKENS // TOK_GRP)
    tenant_of_row = jax.vmap(lambda own, number: assign_block(jax.random.fold_in(part_keys[5], 2), own, number, TOK_GRP, TENANTS, 1, CAP, 2))(tenant_of_row_keys, tenant_of_row_turns).reshape((TOKENS, 1))
    return {"gate_in": gate_in, "up_in": up_in, "down_weight": down_weight, "delta_tiles": delta_tiles, "delta_cols": delta_cols, "tenant_of_row": tenant_of_row}


def reference(gate_in, up_in, down_weight, delta_tiles, delta_cols, tenant_of_row):
    hidden = (jax.nn.silu(gate_in.astype(jnp.float32)) * up_in.astype(jnp.float32)).astype(jnp.bfloat16)
    tenant = tenant_of_row[:, 0].astype(jnp.int32)
    nblk = FF // (128 * N_TENSOR)
    width = nblk * 128
    ncol = D // 128
    place = (delta_cols[..., None] == jnp.arange(ncol, dtype=jnp.int32)).astype(jnp.float32)

    def shard_term(total, s):
        h_s = lax.dynamic_slice_in_dim(hidden, s * width, width, 1)
        w_s = lax.dynamic_slice_in_dim(down_weight, s * width, width, 0)
        base = jnp.dot(h_s, w_s, preferred_element_type=jnp.float32)
        t_s = lax.dynamic_slice_in_dim(delta_tiles, s * nblk, nblk, 1)
        p_s = lax.dynamic_slice_in_dim(place, s * nblk, nblk, 1)

        def group_delta(g):
            start = (g * TOK_GRP).astype(jnp.int32)
            h_g = lax.dynamic_slice_in_dim(h_s, start, TOK_GRP, 0).astype(jnp.float32).reshape(TOK_GRP, nblk, 128)
            ten_g = lax.dynamic_slice_in_dim(tenant, start, TOK_GRP, 0)
            tiles_g = jnp.take(t_s, ten_g, axis=0).astype(jnp.float32)
            place_g = jnp.take(p_s, ten_g, axis=0)
            prods = jnp.einsum('srk,srjkc->srjc', h_g, tiles_g, precision=lax.Precision.HIGHEST)
            spread = jnp.einsum('srjc,srjn->snc', prods, place_g, precision=lax.Precision.HIGHEST)
            return spread.reshape(TOK_GRP, D)

        delta = lax.map(group_delta, jnp.arange(N_ROWS, dtype=jnp.int32)).reshape(TOKENS, D)
        delta = lax.optimization_barrier(delta.astype(jnp.bfloat16))
        term = (base + delta.astype(jnp.float32)).astype(jnp.bfloat16)
        term = lax.optimization_barrier(term)
        return total + term.astype(jnp.float32), None

    start_total = jnp.zeros((TOKENS, D), jnp.float32)
    total, _ = lax.scan(shard_term, start_total, jnp.arange(N_TENSOR, dtype=jnp.int32))
    return total.astype(jnp.bfloat16)
```

```python
import functools

import jax
import jax.numpy as jnp
from jax import lax
from jax.experimental import pallas as pl
from jax.experimental.pallas import tpu as pltpu
from jax.sharding import PartitionSpec as P

BF = jnp.bfloat16
F32 = jnp.float32
LANES = 128
VMEM_LIMIT = 48 * 1024 * 1024


def params():
    return pltpu.CompilerParams(vmem_limit_bytes=VMEM_LIMIT)


def whole():
    return pl.BlockSpec(memory_space=pltpu.VMEM)


def smem():
    return pl.BlockSpec(memory_space=pltpu.SMEM)


def hidden_kernel(gate_ref, up_ref, tenant_ref, out_ref):
    feats = gate_ref.shape[1]
    for start in range(0, feats, 512):
        at = pl.ds(start, min(512, feats - start))
        v = gate_ref[:, at].astype(F32)
        out_ref[:, at] = (v / (1.0 + jnp.exp(-v)) * up_ref[:, at].astype(F32)).astype(BF)
    count = out_ref.shape[0]
    out_ref[:, feats:] = jnp.broadcast_to(tenant_ref[...].astype(F32), (count, LANES)).astype(BF)


def hidden_of(gate, up, tenant):
    count, feats = gate.shape
    return pl.pallas_call(
        hidden_kernel,
        out_shape=jax.ShapeDtypeStruct((count, feats + LANES), BF),
        in_specs=[whole()] * 3,
        out_specs=whole(),
        compiler_params=params(),
        name="hidden",
        cost_estimate=pl.CostEstimate(
            flops=6 * count * feats, bytes_accessed=6 * count * feats, transcendentals=count * feats
        ),
    )(gate, up, tenant)


def slots_of(tenants, tenant):
    count = tenants.shape[0]
    mine = tenants == tenant.astype(F32)
    ones = jnp.where(mine, 1.0, 0.0).astype(BF)
    above = lax.broadcasted_iota(jnp.int32, (count, count), 0) > lax.broadcasted_iota(
        jnp.int32, (count, count), 1
    )
    earlier = jnp.dot(jnp.where(above, 1.0, 0.0).astype(BF), ones, preferred_element_type=F32)
    return jnp.where(mine, earlier, -1024.0)


def one_hot(slots, offset):
    lanes = lax.broadcasted_iota(jnp.int32, slots.shape, 1).astype(F32)
    return jnp.where(slots + offset == lanes, 1.0, 0.0).astype(BF)


def tenant_lanes(hidden_ref):
    return hidden_ref[:, hidden_ref.shape[1] - LANES :].astype(F32)


def delta_kernel(own, cap, bw, chunk, meta_ref, cols_ref, a_ref, b_ref, tiles_ref, *rest):
    outs, (packed, acc) = rest[:-2], rest[-2:]
    step = pl.program_id(0)
    feats = packed.shape[1]
    per_row = tiles_ref.shape[1]
    me = meta_ref[0]
    chip = me // 2

    @pl.when(step == 0)
    def _():
        hot = jnp.concatenate(
            [
                one_hot(slots_of(tenant_lanes(a_ref), me), 0),
                one_hot(slots_of(tenant_lanes(b_ref), me), cap),
            ],
            axis=0,
        )
        for start in range(0, feats, 512):
            at = pl.ds(start, min(512, feats - start))
            both = jnp.concatenate([a_ref[:, at], b_ref[:, at]], axis=0)
            rows = lax.dot_general(hot, both, (((0,), (0,)), ((), ())), preferred_element_type=F32)
            packed[:, at] = rows[: 2 * cap].astype(BF)
        acc[...] = jnp.zeros_like(acc)

    for block in range(chunk):
        row = step * chunk + block
        lhs = packed[:, pl.ds(pl.multiple_of(row * LANES, LANES), LANES)]
        rhs = jnp.concatenate([tiles_ref[block, j] for j in range(per_row)], axis=1)
        prods = jnp.dot(lhs, rhs, preferred_element_type=F32)
        at = [cols_ref[row * per_row + j] for j in range(per_row)]
        old = [acc[at[j]] for j in range(per_row)]
        for j in range(per_row):
            acc[at[j]] = old[j] + prods[:, j * LANES : (j + 1) * LANES]

    ncol = acc.shape[0]
    tiles = bw // LANES
    pairs = ncol // (2 * tiles)

    @pl.when(step == pl.num_programs(0) - 1)
    def _():
        if own:
            for n in range(ncol):
                got = acc[n].astype(F32)
                for g in range(2):
                    outs[g][:, n * LANES : (n + 1) * LANES] = got[g * cap : (g + 1) * cap].astype(BF)
        else:
            for n in range(tiles):
                at = slice(n * LANES, (n + 1) * LANES)
                outs[0][:, at] = acc[me * tiles + n].astype(BF)
                outs[1][:, at] = acc[(me + 1 - 2 * (me % 2)) * tiles + n].astype(BF)
            for e in range(1, pairs):
                first = lax.rem(chip + e, pairs) * 2 * tiles
                for n in range(2 * tiles):
                    got = acc[first + n]
                    to = (e - 1) * 2 * tiles + n
                    for g in range(2):
                        outs[2 + g][:, to * LANES : (to + 1) * LANES] = got[
                            g * cap : (g + 1) * cap
                        ].astype(BF)


def delta_of(own, cap, groups, width, meta, cols, a, b, tiles):
    nblk, per_row = tiles.shape[:2]
    feats = nblk * LANES
    bw = width // groups
    chunk = min(4, nblk)
    far = width - 2 * bw
    if own:
        shapes = [(cap, width)] * 2
    else:
        shapes = [(2 * cap, bw)] * 2 + [(cap, far)] * 2
    rows = 2 * cap
    full = lambda s: pl.BlockSpec(s, lambda i, *_: (0,) * len(s))
    return pl.pallas_call(
        functools.partial(delta_kernel, own, cap, bw, chunk),
        grid_spec=pltpu.PrefetchScalarGridSpec(
            num_scalar_prefetch=2,
            grid=(nblk // chunk,),
            in_specs=[
                full(a.shape),
                full(b.shape),
                pl.BlockSpec((chunk, per_row, LANES, LANES), lambda i, *_: (i, 0, 0, 0)),
            ],
            out_specs=[full(s) for s in shapes],
            scratch_shapes=[
                pltpu.VMEM((rows, feats), BF),
                pltpu.VMEM((width // LANES, rows, LANES), F32),
            ],
        ),
        out_shape=[jax.ShapeDtypeStruct(s, BF) for s in shapes],
        compiler_params=params(),
        name="delta_own" if own else "delta_far",
        cost_estimate=pl.CostEstimate(
            flops=2 * rows * nblk * per_row * LANES * LANES * 4,
            bytes_accessed=2 * tiles.size + 4 * a.size,
            transcendentals=0,
        ),
    )(meta, cols, a, b, tiles)


def base_kernel(merge, cap, meta_ref, a_ref, b_ref, w_ref, *rest):
    if merge:
        mine_ref, other_ref, ca_ref, cb_ref, both, hot = rest
    else:
        ca_ref, cb_ref, both = rest
    count = a_ref.shape[0]
    feats = w_ref.shape[0]

    @pl.when(pl.program_id(0) == 0)
    def _():
        both[:count] = a_ref[:, :feats]
        both[count:] = b_ref[:, :feats]
        if merge:
            me = meta_ref[0]
            mate = me + 1 - 2 * (me % 2)
            for g, ref in enumerate((a_ref, b_ref)):
                tenants = tenant_lanes(ref)
                mine = one_hot(slots_of(tenants, me), g * cap)
                other = one_hot(slots_of(tenants, mate), (1 - g) * cap)
                hot[0, g * count : (g + 1) * count] = mine
                hot[1, g * count : (g + 1) * count] = other

    total = jnp.dot(both[...], w_ref[...], preferred_element_type=F32)
    if merge:
        total += jnp.dot(hot[0][:, : 2 * cap], mine_ref[...], preferred_element_type=F32)
        total += jnp.dot(hot[1][:, : 2 * cap], other_ref[...], preferred_element_type=F32)
    ca_ref[...] = total[:count].astype(BF)
    cb_ref[...] = total[count:].astype(BF)


def base_of(cap, meta, a, b, weight, mine=None, other=None):
    count = a.shape[0]
    feats, bw = weight.shape
    bn = min(256, bw)
    merge = mine is not None
    full = lambda s: pl.BlockSpec(s, lambda i, *_: (0,) * len(s))
    scratch = [pltpu.VMEM((2 * count, feats), BF)]
    specs = [full(a.shape), full(b.shape), pl.BlockSpec((feats, bn), lambda i, *_: (0, i))]
    args = [a, b, weight]
    if merge:
        scratch.append(pltpu.VMEM((2, 2 * count, LANES), BF))
        specs += [pl.BlockSpec((2 * cap, bn), lambda i, *_: (0, i))] * 2
        args += [mine, other]
    return pl.pallas_call(
        functools.partial(base_kernel, merge, cap),
        grid_spec=pltpu.PrefetchScalarGridSpec(
            num_scalar_prefetch=1,
            grid=(bw // bn,),
            in_specs=specs,
            out_specs=[pl.BlockSpec((count, bn), lambda i, *_: (0, i))] * 2,
            scratch_shapes=scratch,
        ),
        out_shape=[jax.ShapeDtypeStruct((count, bw), BF)] * 2,
        compiler_params=params(),
        name="base_far" if merge else "base_own",
        cost_estimate=pl.CostEstimate(
            flops=4 * count * feats * bw, bytes_accessed=2 * weight.size + 4 * a.size, transcendentals=0
        ),
    )(meta, *args)


def merge_kernel(cap, groups, nz, meta_ref, own_ref, dself_ref, dmate_ref, cself_ref, cmate_ref, *rest):
    pairs = groups // 2
    far = rest[: 4 * (pairs - 1)]
    outs, acc = rest[4 * (pairs - 1) : -1], rest[-1]
    me, z = meta_ref[0], meta_ref[1]
    mate = me + 1 - 2 * (me % 2)
    chip = me // 2
    width = acc.shape[1]
    bw = width // groups
    tenants = tenant_lanes(own_ref)

    def hot(tenant, offset):
        return one_hot(slots_of(tenants, tenant), offset)

    near = (hot(me, 0) + hot(mate, cap))[:, : 2 * cap]
    step = min(512, bw)
    for start in range(0, width, step):
        at = pl.ds(start, step)
        rows = jnp.concatenate([dself_ref[:, at].astype(F32), dmate_ref[:, at].astype(F32)], axis=0)
        acc[:, at] = jnp.dot(near, rows.astype(BF), preferred_element_type=F32)

    def add(block, piece):
        at = pl.ds(pl.multiple_of(block * bw, LANES), bw)
        acc[:, at] += piece[...].astype(F32)

    add(me, cself_ref)
    add(mate, cmate_ref)
    for dx in range(1, pairs):
        c_same, c_diag, d_same, d_diag = far[4 * (dx - 1) : 4 * dx]
        source = lax.rem(chip + pairs - dx, pairs)
        same = 2 * source + me % 2
        diag = 2 * source + 1 - me % 2
        add(same, c_same)
        add(diag, c_diag)
        there = (hot(same, 0) + hot(diag, cap))[:, : 2 * cap]
        for e in range(1, pairs):
            target = lax.rem(source + e, pairs)
            for start in range(0, 2 * bw, step):
                at = pl.ds((e - 1) * 2 * bw + start, step)
                rows = jnp.concatenate([d_same[:, at].astype(F32), d_diag[:, at].astype(F32)], axis=0)
                to = pl.ds(pl.multiple_of(target * 2 * bw + start, LANES), step)
                acc[:, to] += jnp.dot(there, rows.astype(BF), preferred_element_type=F32)

    zw = width // nz
    if len(outs) == nz:
        for dz in range(nz):
            block = lax.rem(z + dz, nz)
            at = pl.ds(pl.multiple_of(block * zw, LANES), zw)
            outs[dz][...] = acc[:, at].astype(outs[dz].dtype)
    else:
        outs[0][...] = acc[...].astype(BF)


def merge_of(cap, groups, nz, direct, width, meta, own, *pieces):
    count = own.shape[0]
    zw = width // nz
    if direct:
        shapes = [jax.ShapeDtypeStruct((count, zw), F32 if dz == 0 else BF) for dz in range(nz)]
    else:
        shapes = [jax.ShapeDtypeStruct((count, width), BF)]
    return pl.pallas_call(
        functools.partial(merge_kernel, cap, groups, nz),
        out_shape=shapes,
        in_specs=[smem()] + [whole()] * (1 + len(pieces)),
        out_specs=[whole()] * len(shapes),
        scratch_shapes=[pltpu.VMEM((count, width), F32)],
        compiler_params=params(),
        name="merge",
        cost_estimate=pl.CostEstimate(
            flops=4 * count * width * LANES, bytes_accessed=8 * count * width, transcendentals=0
        ),
    )(meta, own, *pieces)


def shards(groups, nz, gate_in, up_in, down_weight, delta_tiles, delta_cols, tenant_of_row):
    count = gate_in.shape[0]
    pairs = groups // 2
    bw = down_weight.shape[1]
    width = bw * groups
    cap = -(-(count * 3 // (2 * groups)) // 8) * 8
    meta = jnp.stack([lax.axis_index("rows"), lax.axis_index("tensor")]).astype(jnp.int32)
    cols = delta_cols.reshape(-1)
    tiles = delta_tiles[0]

    def rows_to(pick):
        return [(2 * x + c, pick(x, c)) for x in range(pairs) for c in range(2)]

    swap = rows_to(lambda x, c: 2 * x + 1 - c)

    def back(dx):
        return rows_to(lambda x, c: 2 * ((x - dx) % pairs) + c)

    def ahead(dx, cross):
        return rows_to(lambda x, c: 2 * ((x + dx) % pairs) + (1 - c if cross else c))

    def permute(v, perm):
        return lax.ppermute(v, "rows", perm)

    own = hidden_of(gate_in, up_in, tenant_of_row)
    away = [permute(own, back(dx)) for dx in range(1, pairs)]
    mate = permute(own, swap)
    d_self, d_mate = delta_of(True, cap, groups, width, meta, cols, own, mate, tiles)
    d_near = permute(d_mate, swap)
    c_self, c_mate = base_of(cap, meta, own, mate, down_weight)
    c_near = permute(c_mate, swap)
    pieces = [d_self, d_near, c_self, c_near]
    for dx in range(1, pairs):
        same = away[dx - 1]
        diag = permute(same, swap)
        mine, other, d_same, d_diag = delta_of(
            False, cap, groups, width, meta, cols, same, diag, tiles
        )
        other = permute(other, swap)
        d_same = permute(d_same, ahead(dx, False))
        d_diag = permute(d_diag, ahead(dx, True))
        c_same, c_diag = base_of(cap, meta, same, diag, down_weight, mine, other)
        c_same = permute(c_same, ahead(dx, False))
        c_diag = permute(c_diag, ahead(dx, True))
        pieces += [c_same, c_diag, d_same, d_diag]
    direct = nz <= 4
    terms = merge_of(cap, groups, nz, direct, width, meta, own, *pieces)
    if not direct:
        return lax.psum_scatter(terms[0], "tensor", scatter_dimension=1, tiled=True)
    total = terms[0]
    for dz in range(1, nz):
        perm = [(z, (z + dz) % nz) for z in range(nz)]
        total = total + lax.ppermute(terms[dz], "tensor", perm).astype(F32)
    return total.astype(BF)


def solution(mesh):
    groups, nz = mesh.shape["rows"], mesh.shape["tensor"]
    return jax.shard_map(
        functools.partial(shards, groups, nz),
        mesh=mesh,
        in_specs=(
            P(("replica", "rows"), "tensor"),
            P(("replica", "rows"), "tensor"),
            P("tensor", "rows"),
            P("rows", "tensor", None, None, None),
            P("rows", "tensor", None),
            P(("replica", "rows"), None),
        ),
        out_specs=P(("replica", "rows"), "tensor"),
        check_vma=False,
    )
```

```python
import functools

import jax
import jax.numpy as jnp
from jax import lax
from jax.experimental import pallas as pl
from jax.experimental.pallas import tpu as pltpu
from jax.sharding import PartitionSpec as P

BF = jnp.bfloat16
F32 = jnp.float32
LANES = 128
VMEM_LIMIT = 28 * 1024 * 1024
PARTS = 2


def params():
    return pltpu.CompilerParams(vmem_limit_bytes=VMEM_LIMIT)


def whole():
    return pl.BlockSpec(memory_space=pltpu.VMEM)


def smem():
    return pl.BlockSpec(memory_space=pltpu.SMEM)


def hidden_kernel(tenant_ref, gate_ref, up_ref, out_ref):
    width = gate_ref.shape[1]
    count, total = out_ref.shape
    step = pl.program_id(0)
    for start in range(0, width, 512):
        at = pl.ds(start, min(512, width - start))
        v = gate_ref[:, at].astype(F32)
        to = pl.ds(pl.multiple_of(step * width + start, LANES), min(512, width - start))
        out_ref[:, to] = (v / (1.0 + jnp.exp(-v)) * up_ref[:, at].astype(F32)).astype(BF)

    @pl.when(step == 0)
    def _():
        row = jnp.broadcast_to(tenant_ref[...].astype(F32), (count, count))
        diagonal = lax.broadcasted_iota(jnp.int32, (count, count), 0) == lax.broadcasted_iota(
            jnp.int32, (count, count), 1
        )
        column = jnp.sum(jnp.where(diagonal, row, 0.0), axis=1, keepdims=True)
        out_ref[:, total - LANES :] = jnp.broadcast_to(column, (count, LANES)).astype(BF)


def hidden_of(gate, up, tenant):
    count, feats = gate.shape
    steps = 4 if feats % (4 * LANES) == 0 else 1
    part = pl.BlockSpec((count, feats // steps), lambda i: (0, i))
    return pl.pallas_call(
        hidden_kernel,
        grid=(steps,),
        out_shape=jax.ShapeDtypeStruct((count, feats + LANES), BF),
        in_specs=[pl.BlockSpec((1, count), lambda i: (0, 0)), part, part],
        out_specs=pl.BlockSpec((count, feats + LANES), lambda i: (0, 0)),
        compiler_params=params(),
        name="hidden",
        cost_estimate=pl.CostEstimate(
            flops=6 * count * feats, bytes_accessed=6 * count * feats, transcendentals=count * feats
        ),
    )(tenant.reshape(1, count), gate, up)


def slots_of(tenants, tenant):
    count = tenants.shape[0]
    mine = tenants == tenant.astype(F32)
    ones = jnp.where(mine, 1.0, 0.0).astype(BF)
    above = lax.broadcasted_iota(jnp.int32, (count, count), 0) > lax.broadcasted_iota(
        jnp.int32, (count, count), 1
    )
    earlier = jnp.dot(jnp.where(above, 1.0, 0.0).astype(BF), ones, preferred_element_type=F32)
    return jnp.where(mine, earlier, -1024.0)


def one_hot(slots, offset):
    lanes = lax.broadcasted_iota(jnp.int32, slots.shape, 1).astype(F32)
    return jnp.where(slots + offset == lanes, 1.0, 0.0).astype(BF)


def tenant_lanes(hidden_ref):
    return hidden_ref[:, hidden_ref.shape[1] - LANES :].astype(F32)


def pack_rows(cap, me, a_ref, b_ref, packed):
    feats = packed.shape[1]
    hot = jnp.concatenate(
        [
            one_hot(slots_of(tenant_lanes(a_ref), me), 0),
            one_hot(slots_of(tenant_lanes(b_ref), me), cap),
        ],
        axis=0,
    )
    for start in range(0, feats, 512):
        at = pl.ds(start, min(512, feats - start))
        both = jnp.concatenate([a_ref[:, at], b_ref[:, at]], axis=0)
        rows = lax.dot_general(hot, both, (((0,), (0,)), ((), ())), preferred_element_type=F32)
        packed[:, at] = rows[: 2 * cap].astype(BF)


def add_tiles(first, last, cols_ref, packed, tiles_ref, acc):
    per_row = tiles_ref.shape[1]
    for row in range(first, last):
        lhs = packed[:, row * LANES : (row + 1) * LANES]
        rhs = jnp.concatenate([tiles_ref[row, j] for j in range(per_row)], axis=1)
        prods = jnp.dot(lhs, rhs, preferred_element_type=F32)
        at = [cols_ref[row * per_row + j] for j in range(per_row)]
        old = [acc[at[j]] for j in range(per_row)]
        for j in range(per_row):
            acc[at[j]] = old[j] + prods[:, j * LANES : (j + 1) * LANES]


def near_kernel(cap, nt, nw, *refs):
    meta_ref, cols_ref, a_ref, b_ref, tiles_ref, w_ref = refs[:6]
    da_ref, db_ref, ca_ref, cb_ref, tv_ref, wv_ref = refs[6:12]
    packed, acc, both, tsem, wsem = refs[12:]
    count = a_ref.shape[0]
    feats, bw = w_ref.shape
    nblk = tiles_ref.shape[0]
    tpart, wpart = nblk // nt, bw // nw
    tcopies = [
        pltpu.make_async_copy(
            tiles_ref.at[pl.ds(i * tpart, tpart)], tv_ref.at[pl.ds(i * tpart, tpart)], tsem.at[i]
        )
        for i in range(nt)
    ]
    wcopies = [
        pltpu.make_async_copy(
            w_ref.at[:, pl.ds(i * wpart, wpart)], wv_ref.at[:, pl.ds(i * wpart, wpart)], wsem.at[i]
        )
        for i in range(nw)
    ]
    for copy in tcopies + wcopies:
        copy.start()
    pack_rows(cap, meta_ref[0], a_ref, b_ref, packed)
    acc[...] = jnp.zeros_like(acc)
    both[:count] = a_ref[:, :feats]
    both[count:] = b_ref[:, :feats]
    for i in range(nt):
        tcopies[i].wait()
        add_tiles(i * tpart, (i + 1) * tpart, cols_ref, packed, tv_ref, acc)
    for n in range(acc.shape[0]):
        got = acc[n]
        da_ref[:, n * LANES : (n + 1) * LANES] = got[:cap].astype(BF)
        db_ref[:, n * LANES : (n + 1) * LANES] = got[cap:].astype(BF)
    for i in range(nw):
        at = slice(i * wpart, (i + 1) * wpart)
        wcopies[i].wait()
        total = jnp.dot(both[...], wv_ref[:, at], preferred_element_type=F32)
        ca_ref[:, at] = total[:count].astype(BF)
        cb_ref[:, at] = total[count:].astype(BF)


def near_of(cap, width, meta, cols, a, b, tiles, weight):
    count = a.shape[0]
    feats, bw = weight.shape
    nblk = tiles.shape[0]
    nt, nw = (4 if nblk % 4 == 0 else 1), max(1, bw // 512)
    any_space = pl.BlockSpec(memory_space=pl.ANY)
    return pl.pallas_call(
        functools.partial(near_kernel, cap, nt, nw),
        in_specs=[smem(), smem(), whole(), whole(), any_space, any_space],
        out_specs=[whole()] * 6,
        out_shape=[
            jax.ShapeDtypeStruct((cap, width), BF),
            jax.ShapeDtypeStruct((cap, width), BF),
            jax.ShapeDtypeStruct((count, bw), BF),
            jax.ShapeDtypeStruct((count, bw), BF),
            pltpu.VMEM(tiles.shape, BF),
            pltpu.VMEM(weight.shape, BF),
        ],
        scratch_shapes=[
            pltpu.VMEM((2 * cap, feats), BF),
            pltpu.VMEM((width // LANES, 2 * cap, LANES), F32),
            pltpu.VMEM((2 * count, feats), BF),
            pltpu.SemaphoreType.DMA((nt,)),
            pltpu.SemaphoreType.DMA((nw,)),
        ],
        compiler_params=params(),
        name="near",
        cost_estimate=pl.CostEstimate(
            flops=4 * count * feats * bw,
            bytes_accessed=4 * weight.size + 4 * tiles.size,
            transcendentals=0,
        ),
    )(meta, cols, a, b, tiles, weight)


def far_kernel(cap, bw, *refs):
    meta_ref, cols_ref, a_ref, b_ref, tiles_ref, own_ref, mate_ref, da_ref, db_ref, packed, acc = refs
    me = meta_ref[0]
    chip = me // 2
    ncol = acc.shape[0]
    tiles = bw // LANES
    pairs = ncol // (2 * tiles)
    pack_rows(cap, me, a_ref, b_ref, packed)
    acc[...] = jnp.zeros_like(acc)
    add_tiles(0, tiles_ref.shape[0], cols_ref, packed, tiles_ref, acc)
    for n in range(tiles):
        at = slice(n * LANES, (n + 1) * LANES)
        mate_ref[:, at] = acc[(me + 1 - 2 * (me % 2)) * tiles + n].astype(BF)
        own_ref[:, at] = acc[me * tiles + n].astype(BF)
        got = []
        for e in range(1, pairs):
            first = lax.rem(chip + e, pairs) * 2 * tiles
            got += [acc[first + n], acc[first + tiles + n]]
        da_ref[:, at] = jnp.concatenate([v[:cap] for v in got], axis=0).astype(BF)
        db_ref[:, at] = jnp.concatenate([v[cap:] for v in got], axis=0).astype(BF)


def far_of(cap, groups, width, meta, cols, a, b, tiles):
    feats = tiles.shape[0] * LANES
    bw = width // groups
    away = (groups - 2) * cap
    return pl.pallas_call(
        functools.partial(far_kernel, cap, bw),
        in_specs=[smem(), smem(), whole(), whole(), whole()],
        out_specs=[whole()] * 4,
        out_shape=[jax.ShapeDtypeStruct((rows, bw), BF) for rows in (2 * cap, 2 * cap, away, away)],
        scratch_shapes=[
            pltpu.VMEM((2 * cap, feats), BF),
            pltpu.VMEM((width // LANES, 2 * cap, LANES), F32),
        ],
        compiler_params=params(),
        name="far",
        cost_estimate=pl.CostEstimate(
            flops=16 * cap * tiles.size, bytes_accessed=2 * tiles.size, transcendentals=0
        ),
    )(meta, cols, a, b, tiles)


def send_kernel(cap, start, *refs):
    meta_ref, a_ref, b_ref, w_ref, mine_ref, other_ref, da_ref, db_ref, ma_ref, mb_ref, both = refs
    count = a_ref.shape[0]
    feats = w_ref.shape[0]
    sub = ma_ref.shape[1]
    both[:count] = a_ref[:, :feats]
    both[count:] = b_ref[:, :feats]
    me = meta_ref[0]
    mate = me + 1 - 2 * (me % 2)
    mine, other = [], []
    for g, ref in enumerate((a_ref, b_ref)):
        tenants = tenant_lanes(ref)
        mine.append(one_hot(slots_of(tenants, me), g * cap)[:, : 2 * cap])
        other.append(one_hot(slots_of(tenants, mate), (1 - g) * cap)[:, : 2 * cap])
    mine, other = jnp.concatenate(mine, axis=0), jnp.concatenate(other, axis=0)
    step = min(256, sub)
    for n in range(0, sub, step):
        at, to = pl.ds(start + n, step), pl.ds(n, step)
        total = jnp.dot(both[...], w_ref[:, at], preferred_element_type=F32)
        total += jnp.dot(mine, mine_ref[:, at], preferred_element_type=F32)
        total += jnp.dot(other, other_ref[:, at], preferred_element_type=F32)
        ma_ref[:count, to] = total[:count].astype(BF)
        mb_ref[:count, to] = total[count:].astype(BF)
    ma_ref[count:] = da_ref[:, pl.ds(start, sub)]
    mb_ref[count:] = db_ref[:, pl.ds(start, sub)]


def send_of(cap, start, sub, meta, a, b, weight, mine, other, da, db):
    count = a.shape[0]
    feats = weight.shape[0]
    rows = count + da.shape[0]
    return pl.pallas_call(
        functools.partial(send_kernel, cap, start),
        in_specs=[smem()] + [whole()] * 7,
        out_specs=[whole()] * 2,
        out_shape=[jax.ShapeDtypeStruct((rows, sub), BF)] * 2,
        scratch_shapes=[pltpu.VMEM((2 * count, feats), BF)],
        compiler_params=params(),
        name="send",
        cost_estimate=pl.CostEstimate(
            flops=4 * count * feats * sub, bytes_accessed=2 * feats * sub, transcendentals=0
        ),
    )(meta, a, b, weight, mine, other, da, db)


def merge_kernel(cap, groups, nz, bw, start, *refs):
    meta_ref, own_ref, dself_ref, dmate_ref, cself_ref, cmate_ref = refs[:6]
    pairs = groups // 2
    far = refs[6 : 6 + 2 * (pairs - 1)]
    outs, acc = refs[6 + 2 * (pairs - 1) : -1], refs[-1]
    sub = acc.shape[2]
    me, z = meta_ref[0], meta_ref[1]
    mate = me + 1 - 2 * (me % 2)
    chip = me // 2
    count = own_ref.shape[0]
    tenants = tenant_lanes(own_ref)
    near = one_hot(slots_of(tenants, me), 0) + one_hot(slots_of(tenants, mate), cap)
    near = near[:, : 2 * cap]
    for block in range(groups):
        at = pl.ds(block * bw + start, sub)
        rows = jnp.concatenate([dself_ref[:, at].astype(F32), dmate_ref[:, at].astype(F32)], axis=0)
        acc[block] = jnp.dot(near, rows.astype(BF), preferred_element_type=F32)
    acc[me] += cself_ref[:, start : start + sub].astype(F32)
    acc[mate] += cmate_ref[:, start : start + sub].astype(F32)
    for dx in range(1, pairs):
        source = lax.rem(chip + pairs - dx, pairs)
        for k, owner in enumerate((2 * source + me % 2, 2 * source + 1 - me % 2)):
            got = far[2 * (dx - 1) + k]
            acc[owner] += got[:count].astype(F32)
            slots = slots_of(tenants, owner)
            delta = got[count:]
            for e in range(1, pairs):
                target = lax.rem(source + e, pairs)
                for half in range(2):
                    row = (2 * (e - 1) + half) * cap
                    hot = one_hot(slots, row)[:, : delta.shape[0]]
                    acc[2 * target + half] += jnp.dot(hot, delta, preferred_element_type=F32)
    if len(outs) == nz:
        for dz in range(nz):
            outs[dz][...] = acc[lax.rem(z + dz, nz)].astype(outs[dz].dtype)
    else:
        for block in range(groups):
            outs[0][:, block * bw : (block + 1) * bw] = acc[block].astype(BF)


def merge_of(cap, groups, nz, direct, bw, start, sub, meta, own, *pieces):
    count = own.shape[0]
    if direct:
        shapes = [jax.ShapeDtypeStruct((count, sub), F32 if dz == 0 else BF) for dz in range(nz)]
    else:
        shapes = [jax.ShapeDtypeStruct((count, groups * bw), BF)]
    return pl.pallas_call(
        functools.partial(merge_kernel, cap, groups, nz, bw, start),
        out_shape=shapes,
        in_specs=[smem()] + [whole()] * (1 + len(pieces)),
        out_specs=[whole()] * len(shapes),
        scratch_shapes=[pltpu.VMEM((groups, count, sub), F32)],
        compiler_params=params(),
        name="merge",
        cost_estimate=pl.CostEstimate(
            flops=4 * count * groups * sub * LANES, bytes_accessed=8 * count * groups * sub, transcendentals=0
        ),
    )(meta, own, *pieces)


def shards(groups, nz, gate_in, up_in, down_weight, delta_tiles, delta_cols, tenant_of_row):
    count = gate_in.shape[0]
    pairs = groups // 2
    bw = down_weight.shape[1]
    width = bw * groups
    cap = -(-(count * 3 // (2 * groups)) // 8) * 8
    direct = nz == groups and nz <= 4
    parts = PARTS if direct else 1
    sub = bw // parts
    meta = jnp.stack([lax.axis_index("rows"), lax.axis_index("tensor")]).astype(jnp.int32)
    cols = delta_cols.reshape(-1)
    tiles = delta_tiles[0]

    def rows_to(pick):
        return [(2 * x + c, pick(x, c)) for x in range(pairs) for c in range(2)]

    swap = rows_to(lambda x, c: 2 * x + 1 - c)

    def back(dx):
        return rows_to(lambda x, c: 2 * ((x - dx) % pairs) + c)

    def ahead(dx, cross):
        return rows_to(lambda x, c: 2 * ((x + dx) % pairs) + (1 - c if cross else c))

    def permute(v, perm):
        return lax.ppermute(v, "rows", perm)

    own = hidden_of(gate_in, up_in, tenant_of_row)
    away = [permute(own, back(dx)) for dx in range(1, pairs)]
    mate = permute(own, swap)
    d_self, d_mate, c_self, c_mate, tiles, weight = near_of(
        cap, width, meta, cols, own, mate, tiles, down_weight
    )
    away, c_self = lax.optimization_barrier((away, c_self))
    d_near = permute(d_mate, swap)
    c_near = permute(c_mate, swap)
    messages = [[] for _ in range(parts)]
    for dx in range(1, pairs):
        same = away[dx - 1]
        diag = permute(same, swap)
        mine, other, d_same, d_diag = far_of(cap, groups, width, meta, cols, same, diag, tiles)
        other = permute(other, swap)
        for part in range(parts):
            m_same, m_diag = send_of(
                cap, part * sub, sub, meta, same, diag, weight, mine, other, d_same, d_diag
            )
            messages[part] += [permute(m_same, ahead(dx, False)), permute(m_diag, ahead(dx, True))]
    out = []
    for part in range(parts):
        terms = merge_of(
            cap, groups, nz, direct, bw, part * sub, sub, meta, own,
            d_self, d_near, c_self, c_near, *messages[part],
        )
        if not direct:
            return lax.psum_scatter(terms[0], "tensor", scatter_dimension=1, tiled=True)
        total = terms[0]
        for dz in range(1, nz):
            perm = [(z, (z + dz) % nz) for z in range(nz)]
            total = total + lax.ppermute(terms[dz], "tensor", perm).astype(F32)
        out.append(total.astype(BF))
    return jnp.concatenate(out, axis=1)


def solution(mesh):
    groups, nz = mesh.shape["rows"], mesh.shape["tensor"]
    return jax.shard_map(
        functools.partial(shards, groups, nz),
        mesh=mesh,
        in_specs=(
            P(("replica", "rows"), "tensor"),
            P(("replica", "rows"), "tensor"),
            P("tensor", "rows"),
            P("rows", "tensor", None, None, None),
            P("rows", "tensor", None),
            P(("replica", "rows"), None),
        ),
        out_specs=P(("replica", "rows"), "tensor"),
        check_vma=False,
    )
```

```python
import functools

import jax
import jax.numpy as jnp
from jax import lax
from jax.experimental import pallas as pl
from jax.experimental.pallas import tpu as pltpu
from jax.sharding import PartitionSpec as P

BF = jnp.bfloat16
F32 = jnp.float32
LANES = 128
VMEM_LIMIT = 16 * 1024 * 1024
PARTS = (6, 5, 5)


def params():
    return pltpu.CompilerParams(vmem_limit_bytes=VMEM_LIMIT)


def whole():
    return pl.BlockSpec(memory_space=pltpu.VMEM)


def smem():
    return pl.BlockSpec(memory_space=pltpu.SMEM)


def hidden_kernel(chunks, tenant_hbm, gate_hbm, up_hbm, out_ref, tenant_ref, gate_ref, up_ref, sem):
    count, feats = gate_ref.shape
    rows = count // chunks
    copies = [pltpu.make_async_copy(tenant_hbm, tenant_ref, sem.at[2 * chunks])]
    for i in range(chunks):
        at = pl.ds(i * rows, rows)
        copies.append(pltpu.make_async_copy(gate_hbm.at[at], gate_ref.at[at], sem.at[2 * i]))
        copies.append(pltpu.make_async_copy(up_hbm.at[at], up_ref.at[at], sem.at[2 * i + 1]))
    for copy in copies:
        copy.start()
    copies[0].wait()
    row = jnp.broadcast_to(tenant_ref[...].astype(F32), (count, count))
    diagonal = lax.broadcasted_iota(jnp.int32, (count, count), 0) == lax.broadcasted_iota(
        jnp.int32, (count, count), 1
    )
    column = jnp.sum(jnp.where(diagonal, row, 0.0), axis=1, keepdims=True)
    out_ref[:, feats:] = jnp.broadcast_to(column, (count, LANES)).astype(BF)
    for i in range(chunks):
        copies[2 * i + 1].wait()
        copies[2 * i + 2].wait()
        at = pl.ds(i * rows, rows)
        for start in range(0, feats, 512):
            to = pl.ds(start, min(512, feats - start))
            v = gate_ref[at, to].astype(F32)
            out_ref[at, to] = (v / (1.0 + jnp.exp(-v)) * up_ref[at, to].astype(F32)).astype(BF)


def hidden_of(gate, up, tenant):
    count, feats = gate.shape
    chunks = 4 if count % 64 == 0 else 1
    return pl.pallas_call(
        functools.partial(hidden_kernel, chunks),
        out_shape=jax.ShapeDtypeStruct((count, feats + LANES), BF),
        in_specs=[pl.BlockSpec(memory_space=pltpu.HBM)] * 3,
        out_specs=whole(),
        scratch_shapes=[
            pltpu.VMEM((1, count), jnp.int32),
            pltpu.VMEM((count, feats), BF),
            pltpu.VMEM((count, feats), BF),
            pltpu.SemaphoreType.DMA((2 * chunks + 1,)),
        ],
        compiler_params=params(),
        name="hidden",
        cost_estimate=pl.CostEstimate(
            flops=6 * count * feats, bytes_accessed=6 * count * feats, transcendentals=count * feats
        ),
    )(tenant, gate, up)


def slots_of(tenants, tenant):
    count = tenants.shape[0]
    mine = tenants == tenant.astype(F32)
    ones = jnp.where(mine, 1.0, 0.0).astype(BF)
    above = lax.broadcasted_iota(jnp.int32, (count, count), 0) > lax.broadcasted_iota(
        jnp.int32, (count, count), 1
    )
    earlier = jnp.dot(jnp.where(above, 1.0, 0.0).astype(BF), ones, preferred_element_type=F32)
    return jnp.where(mine, earlier, -1024.0)


def one_hot(slots, offset):
    lanes = lax.broadcasted_iota(jnp.int32, slots.shape, 1).astype(F32)
    return jnp.where(slots + offset == lanes, 1.0, 0.0).astype(BF)


def tenant_lanes(hidden_ref):
    return hidden_ref[:, hidden_ref.shape[1] - LANES :].astype(F32)


def pack_rows(cap, me, a_ref, b_ref, packed):
    feats = packed.shape[1]
    hot = jnp.concatenate(
        [
            one_hot(slots_of(tenant_lanes(a_ref), me), 0),
            one_hot(slots_of(tenant_lanes(b_ref), me), cap),
        ],
        axis=0,
    )
    for start in range(0, feats, 512):
        at = pl.ds(start, min(512, feats - start))
        both = jnp.concatenate([a_ref[:, at], b_ref[:, at]], axis=0)
        rows = lax.dot_general(hot, both, (((0,), (0,)), ((), ())), preferred_element_type=F32)
        packed[:, at] = rows[: 2 * cap].astype(BF)


def add_tiles(first, last, cols_ref, packed, tiles_ref, acc):
    per_row = tiles_ref.shape[1]
    for row in range(first, last):
        lhs = packed[:, row * LANES : (row + 1) * LANES]
        rhs = jnp.concatenate([tiles_ref[row, j] for j in range(per_row)], axis=1)
        prods = jnp.dot(lhs, rhs, preferred_element_type=F32)
        at = [cols_ref[j, row] for j in range(per_row)]
        old = [acc[at[j]] for j in range(per_row)]
        for j in range(per_row):
            acc[at[j]] = old[j] + prods[:, j * LANES : (j + 1) * LANES]


def near_kernel(cap, nt, nw, *refs):
    meta_ref, cols_ref, a_ref, b_ref, tiles_ref, w_ref = refs[:6]
    da_ref, db_ref, ca_ref, cb_ref, tv_ref, wv_ref = refs[6:12]
    packed, acc, both, tsem, wsem = refs[12:]
    count = a_ref.shape[0]
    feats, bw = w_ref.shape
    nblk = tiles_ref.shape[0]
    tpart, wpart = nblk // nt, bw // nw
    tcopies = [
        pltpu.make_async_copy(
            tiles_ref.at[pl.ds(i * tpart, tpart)], tv_ref.at[pl.ds(i * tpart, tpart)], tsem.at[i]
        )
        for i in range(nt)
    ]
    wcopies = [
        pltpu.make_async_copy(
            w_ref.at[:, pl.ds(i * wpart, wpart)], wv_ref.at[:, pl.ds(i * wpart, wpart)], wsem.at[i]
        )
        for i in range(nw)
    ]
    for copy in tcopies + wcopies:
        copy.start()
    pack_rows(cap, meta_ref[0], a_ref, b_ref, packed)
    acc[...] = jnp.zeros_like(acc)
    both[:count] = a_ref[:, :feats]
    both[count:] = b_ref[:, :feats]
    for i in range(nt):
        tcopies[i].wait()
        add_tiles(i * tpart, (i + 1) * tpart, cols_ref, packed, tv_ref, acc)
    for n in range(acc.shape[0]):
        got = acc[n]
        da_ref[:, n * LANES : (n + 1) * LANES] = got[:cap].astype(BF)
        db_ref[:, n * LANES : (n + 1) * LANES] = got[cap:].astype(BF)
    for i in range(nw):
        at = slice(i * wpart, (i + 1) * wpart)
        wcopies[i].wait()
        total = jnp.dot(both[...], wv_ref[:, at], preferred_element_type=F32)
        ca_ref[:, at] = total[:count].astype(BF)
        cb_ref[:, at] = total[count:].astype(BF)


def near_of(cap, width, meta, cols, a, b, tiles, weight):
    count = a.shape[0]
    feats, bw = weight.shape
    nblk = tiles.shape[0]
    nt, nw = (4 if nblk % 4 == 0 else 1), max(1, bw // 512)
    any_space = pl.BlockSpec(memory_space=pltpu.HBM)
    return pl.pallas_call(
        functools.partial(near_kernel, cap, nt, nw),
        in_specs=[smem(), smem(), whole(), whole(), any_space, any_space],
        out_specs=[whole()] * 6,
        out_shape=[
            jax.ShapeDtypeStruct((cap, width), BF),
            jax.ShapeDtypeStruct((cap, width), BF),
            jax.ShapeDtypeStruct((count, bw), BF),
            jax.ShapeDtypeStruct((count, bw), BF),
            pltpu.VMEM(tiles.shape, BF),
            pltpu.VMEM(weight.shape, BF),
        ],
        scratch_shapes=[
            pltpu.VMEM((2 * cap, feats), BF),
            pltpu.VMEM((width // LANES, 2 * cap, LANES), F32),
            pltpu.VMEM((2 * count, feats), BF),
            pltpu.SemaphoreType.DMA((nt,)),
            pltpu.SemaphoreType.DMA((nw,)),
        ],
        compiler_params=params(),
        name="near",
        cost_estimate=pl.CostEstimate(
            flops=4 * count * feats * bw,
            bytes_accessed=4 * weight.size + 4 * tiles.size,
            transcendentals=0,
        ),
    )(meta, cols, a, b, tiles, weight)


def far_kernel(cap, bw, *refs):
    meta_ref, cols_ref, a_ref, b_ref, tiles_ref, own_ref, mate_ref, da_ref, db_ref, both_ref, packed, acc = refs
    count, feats = a_ref.shape[0], packed.shape[1]
    both_ref[:count] = a_ref[:, :feats]
    both_ref[count:] = b_ref[:, :feats]
    me = meta_ref[0]
    chip = me // 2
    ncol = acc.shape[0]
    tiles = bw // LANES
    pairs = ncol // (2 * tiles)
    pack_rows(cap, me, a_ref, b_ref, packed)
    acc[...] = jnp.zeros_like(acc)
    add_tiles(0, tiles_ref.shape[0], cols_ref, packed, tiles_ref, acc)
    for n in range(tiles):
        at = slice(n * LANES, (n + 1) * LANES)
        mate_ref[:, at] = acc[(me + 1 - 2 * (me % 2)) * tiles + n].astype(BF)
        own_ref[:, at] = acc[me * tiles + n].astype(BF)
        got = []
        for e in range(1, pairs):
            first = lax.rem(chip + e, pairs) * 2 * tiles
            got += [acc[first + n], acc[first + tiles + n]]
        da_ref[:, at] = jnp.concatenate([v[:cap] for v in got], axis=0).astype(BF)
        db_ref[:, at] = jnp.concatenate([v[cap:] for v in got], axis=0).astype(BF)


def far_of(cap, groups, width, meta, cols, a, b, tiles):
    feats = tiles.shape[0] * LANES
    bw = width // groups
    away = (groups - 2) * cap
    return pl.pallas_call(
        functools.partial(far_kernel, cap, bw),
        in_specs=[smem(), smem(), whole(), whole(), whole()],
        out_specs=[whole()] * 5,
        out_shape=[jax.ShapeDtypeStruct((rows, bw), BF) for rows in (2 * cap, 2 * cap, away, away)]
        + [jax.ShapeDtypeStruct((2 * a.shape[0], feats), BF)],
        scratch_shapes=[
            pltpu.VMEM((2 * cap, feats), BF),
            pltpu.VMEM((width // LANES, 2 * cap, LANES), F32),
        ],
        compiler_params=params(),
        name="far",
        cost_estimate=pl.CostEstimate(
            flops=16 * cap * tiles.size, bytes_accessed=2 * tiles.size, transcendentals=0
        ),
    )(meta, cols, a, b, tiles)


def send_kernel(cap, start, *refs):
    meta_ref, ta_ref, tb_ref, both, w_ref, mine_ref, other_ref, da_ref, db_ref, ma_ref, mb_ref = refs
    count = ta_ref.shape[0]
    sub = ma_ref.shape[1]
    me = meta_ref[0]
    mate = me + 1 - 2 * (me % 2)
    mine, other = [], []
    for g, ref in enumerate((ta_ref, tb_ref)):
        tenants = tenant_lanes(ref)
        mine.append(one_hot(slots_of(tenants, me), g * cap)[:, : 2 * cap])
        other.append(one_hot(slots_of(tenants, mate), (1 - g) * cap)[:, : 2 * cap])
    mine, other = jnp.concatenate(mine, axis=0), jnp.concatenate(other, axis=0)
    step = 256 if sub % 256 == 0 else LANES
    for n in range(0, sub, step):
        at, to = pl.ds(start + n, step), pl.ds(n, step)
        total = jnp.dot(both[...], w_ref[:, at], preferred_element_type=F32)
        total += jnp.dot(mine, mine_ref[:, at], preferred_element_type=F32)
        total += jnp.dot(other, other_ref[:, at], preferred_element_type=F32)
        ma_ref[:count, to] = total[:count].astype(BF)
        mb_ref[:count, to] = total[count:].astype(BF)
    ma_ref[count:] = da_ref[:, pl.ds(start, sub)]
    mb_ref[count:] = db_ref[:, pl.ds(start, sub)]


def send_of(cap, start, sub, meta, a, b, both, weight, mine, other, da, db):
    count = a.shape[0]
    feats = weight.shape[0]
    rows = count + da.shape[0]
    return pl.pallas_call(
        functools.partial(send_kernel, cap, start),
        in_specs=[smem()] + [whole()] * 8,
        out_specs=[whole()] * 2,
        out_shape=[jax.ShapeDtypeStruct((rows, sub), BF)] * 2,
        compiler_params=params(),
        name="send",
        cost_estimate=pl.CostEstimate(
            flops=4 * count * feats * sub, bytes_accessed=2 * feats * sub, transcendentals=0
        ),
    )(meta, a, b, both, weight, mine, other, da, db)


def merge_kernel(cap, groups, nz, bw, start, *refs):
    meta_ref, own_ref, dself_ref, dmate_ref, cself_ref, cmate_ref = refs[:6]
    pairs = groups // 2
    far = refs[6 : 6 + 2 * (pairs - 1)]
    outs, acc = refs[6 + 2 * (pairs - 1) : -1], refs[-1]
    sub = acc.shape[2]
    me, z = meta_ref[0], meta_ref[1]
    mate = me + 1 - 2 * (me % 2)
    chip = me // 2
    count = own_ref.shape[0]
    tenants = tenant_lanes(own_ref)
    near = one_hot(slots_of(tenants, me), 0) + one_hot(slots_of(tenants, mate), cap)
    near = near[:, : 2 * cap]
    for block in range(groups):
        at = pl.ds(block * bw + start, sub)
        rows = jnp.concatenate([dself_ref[:, at].astype(F32), dmate_ref[:, at].astype(F32)], axis=0)
        acc[block] = jnp.dot(near, rows.astype(BF), preferred_element_type=F32)
    acc[me] += cself_ref[:, start : start + sub].astype(F32)
    acc[mate] += cmate_ref[:, start : start + sub].astype(F32)
    for dx in range(1, pairs):
        source = lax.rem(chip + pairs - dx, pairs)
        for k, owner in enumerate((2 * source + me % 2, 2 * source + 1 - me % 2)):
            got = far[2 * (dx - 1) + k]
            acc[owner] += got[:count].astype(F32)
            slots = slots_of(tenants, owner)
            delta = got[count:]
            for e in range(1, pairs):
                target = lax.rem(source + e, pairs)
                for half in range(2):
                    row = (2 * (e - 1) + half) * cap
                    hot = one_hot(slots, row)[:, : delta.shape[0]]
                    acc[2 * target + half] += jnp.dot(hot, delta, preferred_element_type=F32)
    if len(outs) == 3:
        near_z = z + 1 - 2 * lax.rem(z, 2)
        outs[0][:count] = acc[near_z].astype(BF)
        outs[0][count:] = acc[lax.rem(near_z + 2, nz)].astype(BF)
        outs[1][...] = acc[z]
        outs[2][...] = acc[lax.rem(z + 2, nz)]
    else:
        for block in range(groups):
            outs[0][:, block * bw : (block + 1) * bw] = acc[block].astype(BF)


def merge_of(cap, groups, nz, direct, bw, start, sub, meta, own, *pieces):
    count = own.shape[0]
    if direct:
        shapes = [jax.ShapeDtypeStruct((2 * count, sub), BF)] + [jax.ShapeDtypeStruct((count, sub), F32)] * 2
    else:
        shapes = [jax.ShapeDtypeStruct((count, groups * bw), BF)]
    return pl.pallas_call(
        functools.partial(merge_kernel, cap, groups, nz, bw, start),
        out_shape=shapes,
        in_specs=[smem()] + [whole()] * (1 + len(pieces)),
        out_specs=[whole()] * len(shapes),
        scratch_shapes=[pltpu.VMEM((groups, count, sub), F32)],
        compiler_params=params(),
        name="merge",
        cost_estimate=pl.CostEstimate(
            flops=4 * count * groups * sub * LANES, bytes_accessed=8 * count * groups * sub, transcendentals=0
        ),
    )(meta, own, *pieces)


def shards(groups, nz, gate_in, up_in, down_weight, delta_tiles, delta_cols, tenant_of_row):
    count = gate_in.shape[0]
    pairs = groups // 2
    bw = down_weight.shape[1]
    width = bw * groups
    cap = -(-(count * 3 // (2 * groups)) // 8) * 8
    direct = nz == groups == 4 and bw % (LANES * sum(PARTS)) == 0
    cuts = [bw * p // sum(PARTS) for p in PARTS] if direct else [bw]
    starts = [sum(cuts[:i]) for i in range(len(cuts))]
    meta = jnp.stack([lax.axis_index("rows"), lax.axis_index("tensor")]).astype(jnp.int32)
    cols = delta_cols[0].T
    tiles = delta_tiles[0]

    def rows_to(pick):
        return [(2 * x + c, pick(x, c)) for x in range(pairs) for c in range(2)]

    swap = rows_to(lambda x, c: 2 * x + 1 - c)

    def back(dx):
        return rows_to(lambda x, c: 2 * ((x - dx) % pairs) + c)

    def ahead(dx, cross):
        return rows_to(lambda x, c: 2 * ((x + dx) % pairs) + (1 - c if cross else c))

    def permute(v, perm):
        return lax.ppermute(v, "rows", perm)

    stay = lambda v: pltpu.with_memory_space_constraint(v, pltpu.HBM)
    own = hidden_of(stay(gate_in), stay(up_in), stay(tenant_of_row.reshape(1, count)))
    away = [permute(own, back(dx)) for dx in range(1, pairs)]
    mate = permute(own, swap)
    d_self, d_mate, c_self, c_mate, tiles, weight = near_of(
        cap, width, meta, cols, own, mate, stay(tiles), stay(down_weight)
    )
    d_near = permute(d_mate, swap)
    c_near = permute(c_mate, swap)
    away, d_near, c_near = lax.optimization_barrier((away, d_near, c_near))
    sent = []

    def send(message, perm):
        if len(sent) >= 2:
            message, sent[-2] = lax.optimization_barrier((message, sent[-2]))
        sent.append(permute(message, perm))

    for dx in range(1, pairs):
        same = away[dx - 1]
        diag = permute(same, swap)
        mine, other, d_same, d_diag, both = far_of(
            cap, groups, width, meta, cols, same, diag, tiles
        )
        other = permute(other, swap)
        for part, (start, sub) in enumerate(zip(starts, cuts)):
            m_same, m_diag = send_of(
                cap, start, sub, meta, same, diag, both, weight, mine, other, d_same, d_diag
            )
            send(m_same, ahead(dx, False))
            send(m_diag, ahead(dx, True))
    out = []
    for part, (start, sub) in enumerate(zip(starts, cuts)):
        got = []
        for dx in range(1, pairs):
            first = 2 * ((dx - 1) * len(cuts) + part)
            got += sent[first : first + 2]
        terms = merge_of(
            cap, groups, nz, direct, bw, start, sub, meta, own,
            d_self, d_near, c_self, c_near, *got,
        )
        if not direct:
            return lax.psum_scatter(terms[0], "tensor", scatter_dimension=1, tiled=True)
        pair = lax.ppermute(terms[0], "tensor", [(z, z ^ 1) for z in range(nz)])
        passed = (terms[2] + pair[count:].astype(F32)).astype(BF)
        passed = lax.ppermute(passed, "tensor", [(z, z ^ 2) for z in range(nz)])
        total = terms[1] + pair[:count].astype(F32) + passed.astype(F32)
        out.append(total.astype(BF))
    return jnp.concatenate(out, axis=1)


def solution(mesh):
    groups, nz = mesh.shape["rows"], mesh.shape["tensor"]
    return jax.shard_map(
        functools.partial(shards, groups, nz),
        mesh=mesh,
        in_specs=(
            P(("replica", "rows"), "tensor"),
            P(("replica", "rows"), "tensor"),
            P("tensor", "rows"),
            P("rows", "tensor", None, None, None),
            P("rows", "tensor", None),
            P(("replica", "rows"), None),
        ),
        out_specs=P(("replica", "rows"), "tensor"),
        check_vma=False,
    )
```

```python
import functools

import jax
import jax.numpy as jnp
from jax import lax
from jax.experimental import pallas as pl
from jax.experimental.pallas import tpu as pltpu
from jax.sharding import PartitionSpec as P

BF = jnp.bfloat16
F32 = jnp.float32
LANES = 128
VMEM_LIMIT = 16 * 1024 * 1024
PARTS = (6, 6, 4)
LAG = 4
ORDER = (1, 2, 3)


def params():
    return pltpu.CompilerParams(vmem_limit_bytes=VMEM_LIMIT)


def whole():
    return pl.BlockSpec(memory_space=pltpu.VMEM)


def smem():
    return pl.BlockSpec(memory_space=pltpu.SMEM)


def hidden_kernel(chunks, tenant_hbm, gate_hbm, up_hbm, out_ref, tenant_ref, gate_ref, up_ref, sem):
    count, feats = gate_ref.shape
    rows = count // chunks
    copies = [pltpu.make_async_copy(tenant_hbm, tenant_ref, sem.at[2 * chunks])]
    for i in range(chunks):
        at = pl.ds(i * rows, rows)
        copies.append(pltpu.make_async_copy(gate_hbm.at[at], gate_ref.at[at], sem.at[2 * i]))
        copies.append(pltpu.make_async_copy(up_hbm.at[at], up_ref.at[at], sem.at[2 * i + 1]))
    for copy in copies:
        copy.start()
    copies[0].wait()
    row = jnp.broadcast_to(tenant_ref[...].astype(F32), (count, count))
    diagonal = lax.broadcasted_iota(jnp.int32, (count, count), 0) == lax.broadcasted_iota(
        jnp.int32, (count, count), 1
    )
    column = jnp.sum(jnp.where(diagonal, row, 0.0), axis=1, keepdims=True)
    out_ref[:, feats:] = jnp.broadcast_to(column, (count, LANES)).astype(BF)
    for i in range(chunks):
        copies[2 * i + 1].wait()
        copies[2 * i + 2].wait()
        at = pl.ds(i * rows, rows)
        for start in range(0, feats, 512):
            to = pl.ds(start, min(512, feats - start))
            v = gate_ref[at, to].astype(F32)
            out_ref[at, to] = (v / (1.0 + jnp.exp(-v)) * up_ref[at, to].astype(F32)).astype(BF)


def hidden_of(gate, up, tenant):
    count, feats = gate.shape
    chunks = 4 if count % 64 == 0 else 1
    return pl.pallas_call(
        functools.partial(hidden_kernel, chunks),
        out_shape=jax.ShapeDtypeStruct((count, feats + LANES), BF),
        in_specs=[pl.BlockSpec(memory_space=pltpu.HBM)] * 3,
        out_specs=whole(),
        scratch_shapes=[
            pltpu.VMEM((1, count), jnp.int32),
            pltpu.VMEM((count, feats), BF),
            pltpu.VMEM((count, feats), BF),
            pltpu.SemaphoreType.DMA((2 * chunks + 1,)),
        ],
        compiler_params=params(),
        name="hidden",
        cost_estimate=pl.CostEstimate(
            flops=6 * count * feats, bytes_accessed=6 * count * feats, transcendentals=count * feats
        ),
    )(tenant, gate, up)


def slots_of(tenants, tenant):
    count = tenants.shape[0]
    mine = tenants == tenant.astype(F32)
    ones = jnp.where(mine, 1.0, 0.0).astype(BF)
    above = lax.broadcasted_iota(jnp.int32, (count, count), 0) > lax.broadcasted_iota(
        jnp.int32, (count, count), 1
    )
    earlier = jnp.dot(jnp.where(above, 1.0, 0.0).astype(BF), ones, preferred_element_type=F32)
    return jnp.where(mine, earlier, -1024.0)


def one_hot(slots, offset):
    lanes = lax.broadcasted_iota(jnp.int32, slots.shape, 1).astype(F32)
    return jnp.where(slots + offset == lanes, 1.0, 0.0).astype(BF)


def tenant_lanes(hidden_ref):
    return hidden_ref[:, hidden_ref.shape[1] - LANES :].astype(F32)


def pack_rows(cap, me, a_ref, b_ref, packed):
    feats = packed.shape[1]
    hot = jnp.concatenate(
        [
            one_hot(slots_of(tenant_lanes(a_ref), me), 0),
            one_hot(slots_of(tenant_lanes(b_ref), me), cap),
        ],
        axis=0,
    )
    for start in range(0, feats, 512):
        at = pl.ds(start, min(512, feats - start))
        both = jnp.concatenate([a_ref[:, at], b_ref[:, at]], axis=0)
        rows = lax.dot_general(hot, both, (((0,), (0,)), ((), ())), preferred_element_type=F32)
        packed[:, at] = rows[: 2 * cap].astype(BF)


def add_tiles(first, last, cols_ref, packed, tiles_ref, acc):
    per_row = tiles_ref.shape[1]
    for row in range(first, last):
        lhs = packed[:, row * LANES : (row + 1) * LANES]
        rhs = jnp.concatenate([tiles_ref[row, j] for j in range(per_row)], axis=1)
        prods = jnp.dot(lhs, rhs, preferred_element_type=F32)
        at = [cols_ref[j, row] for j in range(per_row)]
        old = [acc[at[j]] for j in range(per_row)]
        for j in range(per_row):
            acc[at[j]] = old[j] + prods[:, j * LANES : (j + 1) * LANES]


def owner_hots(cap, pairs, me, own_ref, hot_ref):
    tenants = tenant_lanes(own_ref)
    mate = me + 1 - 2 * (me % 2)
    hot_ref[0] = one_hot(slots_of(tenants, me), 0) + one_hot(slots_of(tenants, mate), cap)
    away = 2 * (pairs - 1)
    for dx in range(1, pairs):
        source = lax.rem(me // 2 + pairs - dx, pairs)
        for k, owner in enumerate((2 * source + me % 2, 2 * source + 1 - me % 2)):
            slots = slots_of(tenants, owner)
            for block in range(away):
                hot_ref[1 + (2 * (dx - 1) + k) * away + block] = one_hot(slots, block * cap)


def near_kernel(cap, nt, nw, *refs):
    meta_ref, cols_ref, a_ref, b_ref, tiles_ref, w_ref = refs[:6]
    da_ref, db_ref, ca_ref, cb_ref, tv_ref, wv_ref, hot_ref = refs[6:13]
    packed, acc, both, tsem, wsem = refs[13:]
    count = a_ref.shape[0]
    feats, bw = w_ref.shape
    nblk = tiles_ref.shape[0]
    tpart, wpart = nblk // nt, bw // nw
    width_pairs = da_ref.shape[1] // (2 * bw)
    tcopies = [
        pltpu.make_async_copy(
            tiles_ref.at[pl.ds(i * tpart, tpart)], tv_ref.at[pl.ds(i * tpart, tpart)], tsem.at[i]
        )
        for i in range(nt)
    ]
    wcopies = [
        pltpu.make_async_copy(
            w_ref.at[:, pl.ds(i * wpart, wpart)], wv_ref.at[:, pl.ds(i * wpart, wpart)], wsem.at[i]
        )
        for i in range(nw)
    ]
    for copy in tcopies + wcopies:
        copy.start()
    pack_rows(cap, meta_ref[0], a_ref, b_ref, packed)
    acc[...] = jnp.zeros_like(acc)
    both[:count] = a_ref[:, :feats]
    both[count:] = b_ref[:, :feats]
    owner_hots(cap, width_pairs, meta_ref[0], a_ref, hot_ref)
    for i in range(nt):
        tcopies[i].wait()
        add_tiles(i * tpart, (i + 1) * tpart, cols_ref, packed, tv_ref, acc)
    for n in range(acc.shape[0]):
        got = acc[n]
        da_ref[:, n * LANES : (n + 1) * LANES] = got[:cap].astype(BF)
        db_ref[:, n * LANES : (n + 1) * LANES] = got[cap:].astype(BF)
    for i in range(nw):
        at = slice(i * wpart, (i + 1) * wpart)
        wcopies[i].wait()
        total = jnp.dot(both[...], wv_ref[:, at], preferred_element_type=F32)
        ca_ref[:, at] = total[:count].astype(BF)
        cb_ref[:, at] = total[count:].astype(BF)


def near_of(cap, width, meta, cols, a, b, tiles, weight):
    count = a.shape[0]
    feats, bw = weight.shape
    nblk = tiles.shape[0]
    nt, nw = (4 if nblk % 4 == 0 else 1), max(1, bw // 512)
    hots = 1 + (width // bw - 2) ** 2
    any_space = pl.BlockSpec(memory_space=pltpu.HBM)
    return pl.pallas_call(
        functools.partial(near_kernel, cap, nt, nw),
        in_specs=[smem(), smem(), whole(), whole(), any_space, any_space],
        out_specs=[whole()] * 7,
        out_shape=[
            jax.ShapeDtypeStruct((cap, width), BF),
            jax.ShapeDtypeStruct((cap, width), BF),
            jax.ShapeDtypeStruct((count, bw), BF),
            jax.ShapeDtypeStruct((count, bw), BF),
            pltpu.VMEM(tiles.shape, BF),
            pltpu.VMEM(weight.shape, BF),
            jax.ShapeDtypeStruct((hots, count, LANES), BF),
        ],
        scratch_shapes=[
            pltpu.VMEM((2 * cap, feats), BF),
            pltpu.VMEM((width // LANES, 2 * cap, LANES), F32),
            pltpu.VMEM((2 * count, feats), BF),
            pltpu.SemaphoreType.DMA((nt,)),
            pltpu.SemaphoreType.DMA((nw,)),
        ],
        compiler_params=params(),
        name="near",
        cost_estimate=pl.CostEstimate(
            flops=4 * count * feats * bw,
            bytes_accessed=4 * weight.size + 4 * tiles.size,
            transcendentals=0,
        ),
    )(meta, cols, a, b, tiles, weight)


def far_kernel(cap, bw, *refs):
    meta_ref, cols_ref, a_ref, b_ref, tiles_ref, own_ref, mate_ref, da_ref, db_ref, both_ref, hot_ref, packed, acc = refs
    count, feats = a_ref.shape[0], packed.shape[1]
    both_ref[:count] = a_ref[:, :feats]
    both_ref[count:] = b_ref[:, :feats]
    me = meta_ref[0]
    chip = me // 2
    ncol = acc.shape[0]
    tiles = bw // LANES
    pairs = ncol // (2 * tiles)
    mate = me + 1 - 2 * (me % 2)
    for g, ref in enumerate((a_ref, b_ref)):
        tenants = tenant_lanes(ref)
        hot_ref[g * count : (g + 1) * count] = one_hot(slots_of(tenants, me), g * cap) + one_hot(
            slots_of(tenants, mate), (3 - g) * cap
        )
    pack_rows(cap, me, a_ref, b_ref, packed)
    acc[...] = jnp.zeros_like(acc)
    add_tiles(0, tiles_ref.shape[0], cols_ref, packed, tiles_ref, acc)
    for n in range(tiles):
        at = slice(n * LANES, (n + 1) * LANES)
        mate_ref[:, at] = acc[(me + 1 - 2 * (me % 2)) * tiles + n].astype(BF)
        own_ref[:, at] = acc[me * tiles + n].astype(BF)
        got = []
        for e in range(1, pairs):
            first = lax.rem(chip + e, pairs) * 2 * tiles
            got += [acc[first + n], acc[first + tiles + n]]
        da_ref[:, at] = jnp.concatenate([v[:cap] for v in got], axis=0).astype(BF)
        db_ref[:, at] = jnp.concatenate([v[cap:] for v in got], axis=0).astype(BF)


def far_of(cap, groups, width, meta, cols, a, b, tiles):
    feats = tiles.shape[0] * LANES
    bw = width // groups
    away = (groups - 2) * cap
    return pl.pallas_call(
        functools.partial(far_kernel, cap, bw),
        in_specs=[smem(), smem(), whole(), whole(), whole()],
        out_specs=[whole()] * 6,
        out_shape=[jax.ShapeDtypeStruct((rows, bw), BF) for rows in (2 * cap, 2 * cap, away, away)]
        + [jax.ShapeDtypeStruct((2 * a.shape[0], n), BF) for n in (feats, LANES)],
        scratch_shapes=[
            pltpu.VMEM((2 * cap, feats), BF),
            pltpu.VMEM((width // LANES, 2 * cap, LANES), F32),
        ],
        compiler_params=params(),
        name="far",
        cost_estimate=pl.CostEstimate(
            flops=16 * cap * tiles.size, bytes_accessed=2 * tiles.size, transcendentals=0
        ),
    )(meta, cols, a, b, tiles)


def send_kernel(cap, start, *refs):
    hot_ref, both, w_ref, mine_ref, other_ref, da_ref, db_ref, ma_ref, mb_ref = refs
    count = both.shape[0] // 2
    sub = ma_ref.shape[1]
    hot = hot_ref[:, : 4 * cap]
    step = 256 if sub % 256 == 0 else LANES
    for n in range(0, sub, step):
        at, to = pl.ds(start + n, step), pl.ds(n, step)
        total = jnp.dot(both[...], w_ref[:, at], preferred_element_type=F32)
        rows = jnp.concatenate([mine_ref[:, at], other_ref[:, at]], axis=0)
        total += jnp.dot(hot, rows, preferred_element_type=F32)
        ma_ref[:count, to] = total[:count].astype(BF)
        mb_ref[:count, to] = total[count:].astype(BF)
    ma_ref[count:] = da_ref[:, pl.ds(start, sub)]
    mb_ref[count:] = db_ref[:, pl.ds(start, sub)]


def send_of(cap, start, sub, hot, both, weight, mine, other, da, db):
    count = both.shape[0] // 2
    feats = weight.shape[0]
    rows = count + da.shape[0]
    return pl.pallas_call(
        functools.partial(send_kernel, cap, start),
        in_specs=[whole()] * 7,
        out_specs=[whole()] * 2,
        out_shape=[jax.ShapeDtypeStruct((rows, sub), BF)] * 2,
        compiler_params=params(),
        name="send",
        cost_estimate=pl.CostEstimate(
            flops=4 * count * feats * sub, bytes_accessed=2 * feats * sub, transcendentals=0
        ),
    )(hot, both, weight, mine, other, da, db)


def merge_kernel(cap, groups, nz, bw, start, *refs):
    meta_ref, hot_ref, dself_ref, dmate_ref, cself_ref, cmate_ref = refs[:6]
    pairs = groups // 2
    far = refs[6 : 6 + 2 * (pairs - 1)]
    outs, acc = refs[6 + 2 * (pairs - 1) : -1], refs[-1]
    sub = acc.shape[2]
    me, z = meta_ref[0], meta_ref[1]
    mate = me + 1 - 2 * (me % 2)
    chip = me // 2
    count = acc.shape[1]
    near = hot_ref[0][:, : 2 * cap]
    for block in range(groups):
        at = pl.ds(block * bw + start, sub)
        rows = jnp.concatenate([dself_ref[:, at].astype(F32), dmate_ref[:, at].astype(F32)], axis=0)
        acc[block] = jnp.dot(near, rows.astype(BF), preferred_element_type=F32)
    acc[me] += cself_ref[:, start : start + sub].astype(F32)
    acc[mate] += cmate_ref[:, start : start + sub].astype(F32)
    away = groups - 2
    for dx in range(1, pairs):
        source = lax.rem(chip + pairs - dx, pairs)
        for k, owner in enumerate((2 * source + me % 2, 2 * source + 1 - me % 2)):
            got = far[2 * (dx - 1) + k]
            acc[owner] += got[:count].astype(F32)
            delta = got[count:]
            for e in range(1, pairs):
                target = lax.rem(source + e, pairs)
                for half in range(2):
                    block = 2 * (e - 1) + half
                    hot = hot_ref[1 + (2 * (dx - 1) + k) * away + block][:, : delta.shape[0]]
                    acc[2 * target + half] += jnp.dot(hot, delta, preferred_element_type=F32)
    if len(outs) == nz:
        for dz in range(nz):
            outs[dz][...] = acc[lax.rem(z + dz, nz)].astype(outs[dz].dtype)
    else:
        for block in range(groups):
            outs[0][:, block * bw : (block + 1) * bw] = acc[block].astype(BF)


def merge_of(cap, groups, nz, direct, bw, start, sub, meta, hot, *pieces):
    count = hot.shape[1]
    if direct:
        shapes = [jax.ShapeDtypeStruct((count, sub), F32 if dz == 0 else BF) for dz in range(nz)]
    else:
        shapes = [jax.ShapeDtypeStruct((count, groups * bw), BF)]
    return pl.pallas_call(
        functools.partial(merge_kernel, cap, groups, nz, bw, start),
        out_shape=shapes,
        in_specs=[smem()] + [whole()] * (1 + len(pieces)),
        out_specs=[whole()] * len(shapes),
        scratch_shapes=[pltpu.VMEM((groups, count, sub), F32)],
        compiler_params=params(),
        name="merge",
        cost_estimate=pl.CostEstimate(
            flops=4 * count * groups * sub * LANES, bytes_accessed=8 * count * groups * sub, transcendentals=0
        ),
    )(meta, hot, *pieces)


def shards(groups, nz, gate_in, up_in, down_weight, delta_tiles, delta_cols, tenant_of_row):
    count = gate_in.shape[0]
    pairs = groups // 2
    bw = down_weight.shape[1]
    width = bw * groups
    cap = -(-(count * 3 // (2 * groups)) // 8) * 8
    direct = nz == groups == 4 and bw % (LANES * sum(PARTS)) == 0
    cuts = [bw * p // sum(PARTS) for p in PARTS] if direct else [bw]
    starts = [sum(cuts[:i]) for i in range(len(cuts))]
    meta = jnp.stack([lax.axis_index("rows"), lax.axis_index("tensor")]).astype(jnp.int32)
    cols = delta_cols[0].T
    tiles = delta_tiles[0]

    def rows_to(pick):
        return [(2 * x + c, pick(x, c)) for x in range(pairs) for c in range(2)]

    swap = rows_to(lambda x, c: 2 * x + 1 - c)

    def back(dx):
        return rows_to(lambda x, c: 2 * ((x - dx) % pairs) + c)

    def ahead(dx, cross):
        return rows_to(lambda x, c: 2 * ((x + dx) % pairs) + (1 - c if cross else c))

    def permute(v, perm):
        return lax.ppermute(v, "rows", perm)

    stay = lambda v: pltpu.with_memory_space_constraint(v, pltpu.HBM)
    own = hidden_of(stay(gate_in), stay(up_in), stay(tenant_of_row.reshape(1, count)))
    away = [permute(own, back(dx)) for dx in range(1, pairs)]
    mate = permute(own, swap)
    d_self, d_mate, c_self, c_mate, tiles, weight, hot = near_of(
        cap, width, meta, cols, own, mate, stay(tiles), stay(down_weight)
    )
    d_near = permute(d_mate, swap)
    c_near = permute(c_mate, swap)
    away, c_self = lax.optimization_barrier((away, c_self))
    sent = []

    def send(message, perm):
        if len(sent) >= LAG:
            message, sent[-LAG] = lax.optimization_barrier((message, sent[-LAG]))
        sent.append(permute(message, perm))

    for dx in range(1, pairs):
        same = away[dx - 1]
        diag = permute(same, swap)
        mine, other, d_same, d_diag, both, far_hot = far_of(
            cap, groups, width, meta, cols, same, diag, tiles
        )
        other = permute(other, swap)
        for part, (start, sub) in enumerate(zip(starts, cuts)):
            m_same, m_diag = send_of(
                cap, start, sub, far_hot, both, weight, mine, other, d_same, d_diag
            )
            send(m_same, ahead(dx, False))
            send(m_diag, ahead(dx, True))
    out = []
    for part, (start, sub) in enumerate(zip(starts, cuts)):
        got = []
        for dx in range(1, pairs):
            first = 2 * ((dx - 1) * len(cuts) + part)
            got += sent[first : first + 2]
        terms = merge_of(
            cap, groups, nz, direct, bw, start, sub, meta, hot,
            d_self, d_near, c_self, c_near, *got,
        )
        if not direct:
            return lax.psum_scatter(terms[0], "tensor", scatter_dimension=1, tiled=True)
        total = terms[0]
        for dz in ORDER:
            perm = [(z, (z + dz) % nz) for z in range(nz)]
            total = total + lax.ppermute(terms[dz], "tensor", perm).astype(F32)
        out.append(total.astype(BF))
    return jnp.concatenate(out, axis=1)


def solution(mesh):
    groups, nz = mesh.shape["rows"], mesh.shape["tensor"]
    return jax.shard_map(
        functools.partial(shards, groups, nz),
        mesh=mesh,
        in_specs=(
            P(("replica", "rows"), "tensor"),
            P(("replica", "rows"), "tensor"),
            P("tensor", "rows"),
            P("rows", "tensor", None, None, None),
            P("rows", "tensor", None),
            P(("replica", "rows"), None),
        ),
        out_specs=P(("replica", "rows"), "tensor"),
        check_vma=False,
    )
```

```python
import functools

import jax
import jax.numpy as jnp
from jax import lax
from jax.experimental import pallas as pl
from jax.experimental.pallas import tpu as pltpu
from jax.sharding import PartitionSpec as P

BF = jnp.bfloat16
F32 = jnp.float32
LANES = 128
VMEM_LIMIT = 16 * 1024 * 1024
PARTS = (2, 3, 3)
LAG = 4
ORDER = (1, 2, 3)


def params():
    return pltpu.CompilerParams(vmem_limit_bytes=VMEM_LIMIT)


def whole():
    return pl.BlockSpec(memory_space=pltpu.VMEM)


def smem():
    return pl.BlockSpec(memory_space=pltpu.SMEM)


def hidden_kernel(chunks, tenant_hbm, gate_hbm, up_hbm, out_ref, tenant_ref, gate_ref, up_ref, sem):
    count, feats = gate_ref.shape
    rows = count // chunks
    copies = [pltpu.make_async_copy(tenant_hbm, tenant_ref, sem.at[2 * chunks])]
    for i in range(chunks):
        at = pl.ds(i * rows, rows)
        copies.append(pltpu.make_async_copy(gate_hbm.at[at], gate_ref.at[at], sem.at[2 * i]))
        copies.append(pltpu.make_async_copy(up_hbm.at[at], up_ref.at[at], sem.at[2 * i + 1]))
    for copy in copies:
        copy.start()
    copies[0].wait()
    row = jnp.broadcast_to(tenant_ref[...].astype(F32), (count, count))
    diagonal = lax.broadcasted_iota(jnp.int32, (count, count), 0) == lax.broadcasted_iota(
        jnp.int32, (count, count), 1
    )
    column = jnp.sum(jnp.where(diagonal, row, 0.0), axis=1, keepdims=True)
    out_ref[:, feats:] = jnp.broadcast_to(column, (count, LANES)).astype(BF)
    for i in range(chunks):
        copies[2 * i + 1].wait()
        copies[2 * i + 2].wait()
        at = pl.ds(i * rows, rows)
        for start in range(0, feats, 512):
            to = pl.ds(start, min(512, feats - start))
            v = gate_ref[at, to].astype(F32)
            out_ref[at, to] = (v / (1.0 + jnp.exp(-v)) * up_ref[at, to].astype(F32)).astype(BF)


def hidden_of(gate, up, tenant):
    count, feats = gate.shape
    chunks = 4 if count % 64 == 0 else 1
    return pl.pallas_call(
        functools.partial(hidden_kernel, chunks),
        out_shape=jax.ShapeDtypeStruct((count, feats + LANES), BF),
        in_specs=[pl.BlockSpec(memory_space=pltpu.HBM)] * 3,
        out_specs=whole(),
        scratch_shapes=[
            pltpu.VMEM((1, count), jnp.int32),
            pltpu.VMEM((count, feats), BF),
            pltpu.VMEM((count, feats), BF),
            pltpu.SemaphoreType.DMA((2 * chunks + 1,)),
        ],
        compiler_params=params(),
        name="hidden",
        cost_estimate=pl.CostEstimate(
            flops=6 * count * feats, bytes_accessed=6 * count * feats, transcendentals=count * feats
        ),
    )(tenant, gate, up)


def slots_of(tenants, tenant):
    count = tenants.shape[0]
    mine = tenants == tenant.astype(F32)
    ones = jnp.where(mine, 1.0, 0.0).astype(BF)
    above = lax.broadcasted_iota(jnp.int32, (count, count), 0) > lax.broadcasted_iota(
        jnp.int32, (count, count), 1
    )
    earlier = jnp.dot(jnp.where(above, 1.0, 0.0).astype(BF), ones, preferred_element_type=F32)
    return jnp.where(mine, earlier, -1024.0)


def one_hot(slots, offset):
    lanes = lax.broadcasted_iota(jnp.int32, slots.shape, 1).astype(F32)
    return jnp.where(slots + offset == lanes, 1.0, 0.0).astype(BF)


def tenant_lanes(hidden_ref):
    return hidden_ref[:, hidden_ref.shape[1] - LANES :].astype(F32)


def pack_rows(cap, me, a_ref, b_ref, packed):
    feats = packed.shape[1]
    hot = jnp.concatenate(
        [
            one_hot(slots_of(tenant_lanes(a_ref), me), 0),
            one_hot(slots_of(tenant_lanes(b_ref), me), cap),
        ],
        axis=0,
    )
    for start in range(0, feats, 512):
        at = pl.ds(start, min(512, feats - start))
        both = jnp.concatenate([a_ref[:, at], b_ref[:, at]], axis=0)
        rows = lax.dot_general(hot, both, (((0,), (0,)), ((), ())), preferred_element_type=F32)
        packed[:, at] = rows[: 2 * cap].astype(BF)


def add_tiles(first, last, cols_ref, packed, tiles_ref, acc):
    per_row = tiles_ref.shape[1]
    for row in range(first, last):
        lhs = packed[:, row * LANES : (row + 1) * LANES]
        rhs = jnp.concatenate([tiles_ref[row, j] for j in range(per_row)], axis=1)
        prods = jnp.dot(lhs, rhs, preferred_element_type=F32)
        at = [cols_ref[j, row] for j in range(per_row)]
        old = [acc[at[j]] for j in range(per_row)]
        for j in range(per_row):
            acc[at[j]] = old[j] + prods[:, j * LANES : (j + 1) * LANES]


def owner_hots(cap, pairs, me, own_ref, hot_ref):
    tenants = tenant_lanes(own_ref)
    mate = me + 1 - 2 * (me % 2)
    hot_ref[0] = one_hot(slots_of(tenants, me), 0) + one_hot(slots_of(tenants, mate), cap)
    away = 2 * (pairs - 1)
    for dx in range(1, pairs):
        source = lax.rem(me // 2 + pairs - dx, pairs)
        for k, owner in enumerate((2 * source + me % 2, 2 * source + 1 - me % 2)):
            slots = slots_of(tenants, owner)
            for block in range(away):
                hot_ref[1 + (2 * (dx - 1) + k) * away + block] = one_hot(slots, block * cap)


def near_kernel(cap, nt, nw, *refs):
    meta_ref, cols_ref, a_ref, b_ref, tiles_ref, w_ref = refs[:6]
    da_ref, db_ref, ca_ref, cb_ref, tv_ref, wv_ref, hot_ref = refs[6:13]
    packed, acc, both, tsem, wsem = refs[13:]
    count = a_ref.shape[0]
    feats, bw = w_ref.shape
    nblk = tiles_ref.shape[0]
    tpart, wpart = nblk // nt, bw // nw
    width_pairs = da_ref.shape[1] // (2 * bw)
    tcopies = [
        pltpu.make_async_copy(
            tiles_ref.at[pl.ds(i * tpart, tpart)], tv_ref.at[pl.ds(i * tpart, tpart)], tsem.at[i]
        )
        for i in range(nt)
    ]
    wcopies = [
        pltpu.make_async_copy(
            w_ref.at[:, pl.ds(i * wpart, wpart)], wv_ref.at[:, pl.ds(i * wpart, wpart)], wsem.at[i]
        )
        for i in range(nw)
    ]
    for copy in tcopies + wcopies:
        copy.start()
    pack_rows(cap, meta_ref[0], a_ref, b_ref, packed)
    acc[...] = jnp.zeros_like(acc)
    both[:count] = a_ref[:, :feats]
    both[count:] = b_ref[:, :feats]
    owner_hots(cap, width_pairs, meta_ref[0], a_ref, hot_ref)
    for i in range(nt):
        tcopies[i].wait()
        add_tiles(i * tpart, (i + 1) * tpart, cols_ref, packed, tv_ref, acc)
    for n in range(acc.shape[0]):
        got = acc[n]
        da_ref[:, n * LANES : (n + 1) * LANES] = got[:cap].astype(BF)
        db_ref[:, n * LANES : (n + 1) * LANES] = got[cap:].astype(BF)
    for i in range(nw):
        at = slice(i * wpart, (i + 1) * wpart)
        wcopies[i].wait()
        total = jnp.dot(both[...], wv_ref[:, at], preferred_element_type=F32)
        ca_ref[:, at] = total[:count].astype(BF)
        cb_ref[:, at] = total[count:].astype(BF)


def near_of(cap, width, meta, cols, a, b, tiles, weight):
    count = a.shape[0]
    feats, bw = weight.shape
    nblk = tiles.shape[0]
    nt, nw = (4 if nblk % 4 == 0 else 1), max(1, bw // 512)
    hots = 1 + (width // bw - 2) ** 2
    any_space = pl.BlockSpec(memory_space=pltpu.HBM)
    return pl.pallas_call(
        functools.partial(near_kernel, cap, nt, nw),
        in_specs=[smem(), smem(), whole(), whole(), any_space, any_space],
        out_specs=[whole()] * 7,
        out_shape=[
            jax.ShapeDtypeStruct((cap, width), BF),
            jax.ShapeDtypeStruct((cap, width), BF),
            jax.ShapeDtypeStruct((count, bw), BF),
            jax.ShapeDtypeStruct((count, bw), BF),
            pltpu.VMEM(tiles.shape, BF),
            pltpu.VMEM(weight.shape, BF),
            jax.ShapeDtypeStruct((hots, count, LANES), BF),
        ],
        scratch_shapes=[
            pltpu.VMEM((2 * cap, feats), BF),
            pltpu.VMEM((width // LANES, 2 * cap, LANES), F32),
            pltpu.VMEM((2 * count, feats), BF),
            pltpu.SemaphoreType.DMA((nt,)),
            pltpu.SemaphoreType.DMA((nw,)),
        ],
        compiler_params=params(),
        name="near",
        cost_estimate=pl.CostEstimate(
            flops=4 * count * feats * bw,
            bytes_accessed=4 * weight.size + 4 * tiles.size,
            transcendentals=0,
        ),
    )(meta, cols, a, b, tiles, weight)


def far_kernel(cap, bw, *refs):
    meta_ref, cols_ref, a_ref, b_ref, tiles_ref, own_ref, mate_ref, da_ref, db_ref, both_ref, hot_ref, packed, acc = refs
    count, feats = a_ref.shape[0], packed.shape[1]
    both_ref[:count] = a_ref[:, :feats]
    both_ref[count:] = b_ref[:, :feats]
    me = meta_ref[0]
    chip = me // 2
    ncol = acc.shape[0]
    tiles = bw // LANES
    pairs = ncol // (2 * tiles)
    mate = me + 1 - 2 * (me % 2)
    for g, ref in enumerate((a_ref, b_ref)):
        tenants = tenant_lanes(ref)
        hot_ref[g * count : (g + 1) * count] = one_hot(slots_of(tenants, me), g * cap) + one_hot(
            slots_of(tenants, mate), (3 - g) * cap
        )
    pack_rows(cap, me, a_ref, b_ref, packed)
    acc[...] = jnp.zeros_like(acc)
    add_tiles(0, tiles_ref.shape[0], cols_ref, packed, tiles_ref, acc)
    for n in range(tiles):
        at = slice(n * LANES, (n + 1) * LANES)
        mate_ref[:, at] = acc[(me + 1 - 2 * (me % 2)) * tiles + n].astype(BF)
        own_ref[:, at] = acc[me * tiles + n].astype(BF)
        got = []
        for e in range(1, pairs):
            first = lax.rem(chip + e, pairs) * 2 * tiles
            got += [acc[first + n], acc[first + tiles + n]]
        da_ref[:, at] = jnp.concatenate([v[:cap] for v in got], axis=0).astype(BF)
        db_ref[:, at] = jnp.concatenate([v[cap:] for v in got], axis=0).astype(BF)


def far_of(cap, groups, width, meta, cols, a, b, tiles):
    feats = tiles.shape[0] * LANES
    bw = width // groups
    away = (groups - 2) * cap
    return pl.pallas_call(
        functools.partial(far_kernel, cap, bw),
        in_specs=[smem(), smem(), whole(), whole(), whole()],
        out_specs=[whole()] * 6,
        out_shape=[jax.ShapeDtypeStruct((rows, bw), BF) for rows in (2 * cap, 2 * cap, away, away)]
        + [jax.ShapeDtypeStruct((2 * a.shape[0], n), BF) for n in (feats, LANES)],
        scratch_shapes=[
            pltpu.VMEM((2 * cap, feats), BF),
            pltpu.VMEM((width // LANES, 2 * cap, LANES), F32),
        ],
        compiler_params=params(),
        name="far",
        cost_estimate=pl.CostEstimate(
            flops=16 * cap * tiles.size, bytes_accessed=2 * tiles.size, transcendentals=0
        ),
    )(meta, cols, a, b, tiles)


def first_kernel(both, w_ref, out_ref):
    sub = out_ref.shape[1]
    step = 256 if sub % 256 == 0 else LANES
    for n in range(0, sub, step):
        at = pl.ds(n, step)
        out_ref[:, at] = jnp.dot(both[...], w_ref[:, at], preferred_element_type=F32)


def first_of(sub, both, weight):
    return pl.pallas_call(
        first_kernel,
        in_specs=[whole()] * 2,
        out_specs=whole(),
        out_shape=jax.ShapeDtypeStruct((both.shape[0], sub), F32),
        compiler_params=params(),
        name="first",
        cost_estimate=pl.CostEstimate(
            flops=2 * both.size * sub, bytes_accessed=2 * weight.shape[0] * sub, transcendentals=0
        ),
    )(both, weight)


def send_kernel(cap, start, *refs):
    hot_ref, both, w_ref, mine_ref, other_ref, da_ref, db_ref, ma_ref, mb_ref = refs
    count = both.shape[0] // 2
    sub = ma_ref.shape[1]
    hot = hot_ref[:, : 4 * cap]
    step = 256 if sub % 256 == 0 else LANES
    for n in range(0, sub, step):
        at, to = pl.ds(start + n, step), pl.ds(n, step)
        if start == 0:
            total = w_ref[:, to]
        else:
            total = jnp.dot(both[...], w_ref[:, at], preferred_element_type=F32)
        rows = jnp.concatenate([mine_ref[:, at], other_ref[:, at]], axis=0)
        total += jnp.dot(hot, rows, preferred_element_type=F32)
        ma_ref[:count, to] = total[:count].astype(BF)
        mb_ref[:count, to] = total[count:].astype(BF)
    ma_ref[count:] = da_ref[:, pl.ds(start, sub)]
    mb_ref[count:] = db_ref[:, pl.ds(start, sub)]


def send_of(cap, start, sub, hot, both, weight, mine, other, da, db):
    count = both.shape[0] // 2
    feats = both.shape[1]
    rows = count + da.shape[0]
    return pl.pallas_call(
        functools.partial(send_kernel, cap, start),
        in_specs=[whole()] * 7,
        out_specs=[whole()] * 2,
        out_shape=[jax.ShapeDtypeStruct((rows, sub), BF)] * 2,
        compiler_params=params(),
        name="send",
        cost_estimate=pl.CostEstimate(
            flops=4 * count * feats * sub, bytes_accessed=2 * feats * sub, transcendentals=0
        ),
    )(hot, both, weight, mine, other, da, db)


def merge_kernel(cap, groups, nz, bw, start, *refs):
    meta_ref, hot_ref, dself_ref, dmate_ref, cself_ref, cmate_ref = refs[:6]
    pairs = groups // 2
    far = refs[6 : 6 + 2 * (pairs - 1)]
    outs, acc = refs[6 + 2 * (pairs - 1) : -1], refs[-1]
    sub = acc.shape[2]
    me, z = meta_ref[0], meta_ref[1]
    mate = me + 1 - 2 * (me % 2)
    chip = me // 2
    count = acc.shape[1]
    near = hot_ref[0][:, : 2 * cap]
    for block in range(groups):
        at = pl.ds(block * bw + start, sub)
        rows = jnp.concatenate([dself_ref[:, at].astype(F32), dmate_ref[:, at].astype(F32)], axis=0)
        acc[block] = jnp.dot(near, rows.astype(BF), preferred_element_type=F32)
    acc[me] += cself_ref[:, start : start + sub].astype(F32)
    acc[mate] += cmate_ref[:, start : start + sub].astype(F32)
    away = groups - 2
    for dx in range(1, pairs):
        source = lax.rem(chip + pairs - dx, pairs)
        for k, owner in enumerate((2 * source + me % 2, 2 * source + 1 - me % 2)):
            got = far[2 * (dx - 1) + k]
            acc[owner] += got[:count].astype(F32)
            delta = got[count:]
            for e in range(1, pairs):
                target = lax.rem(source + e, pairs)
                for half in range(2):
                    block = 2 * (e - 1) + half
                    hot = hot_ref[1 + (2 * (dx - 1) + k) * away + block][:, : delta.shape[0]]
                    acc[2 * target + half] += jnp.dot(hot, delta, preferred_element_type=F32)
    if len(outs) == nz:
        for dz in range(nz):
            outs[dz][...] = acc[lax.rem(z + dz, nz)].astype(outs[dz].dtype)
    else:
        for block in range(groups):
            outs[0][:, block * bw : (block + 1) * bw] = acc[block].astype(BF)


def merge_of(cap, groups, nz, direct, bw, start, sub, meta, hot, *pieces):
    count = hot.shape[1]
    if direct:
        shapes = [jax.ShapeDtypeStruct((count, sub), F32 if dz == 0 else BF) for dz in range(nz)]
    else:
        shapes = [jax.ShapeDtypeStruct((count, groups * bw), BF)]
    return pl.pallas_call(
        functools.partial(merge_kernel, cap, groups, nz, bw, start),
        out_shape=shapes,
        in_specs=[smem()] + [whole()] * (1 + len(pieces)),
        out_specs=[whole()] * len(shapes),
        scratch_shapes=[pltpu.VMEM((groups, count, sub), F32)],
        compiler_params=params(),
        name="merge",
        cost_estimate=pl.CostEstimate(
            flops=4 * count * groups * sub * LANES, bytes_accessed=8 * count * groups * sub, transcendentals=0
        ),
    )(meta, hot, *pieces)


def shards(groups, nz, gate_in, up_in, down_weight, delta_tiles, delta_cols, tenant_of_row):
    count = gate_in.shape[0]
    pairs = groups // 2
    bw = down_weight.shape[1]
    width = bw * groups
    cap = -(-(count * 3 // (2 * groups)) // 8) * 8
    direct = nz == groups == 4 and bw % (LANES * sum(PARTS)) == 0
    cuts = [bw * p // sum(PARTS) for p in PARTS] if direct else [bw]
    starts = [sum(cuts[:i]) for i in range(len(cuts))]
    meta = jnp.stack([lax.axis_index("rows"), lax.axis_index("tensor")]).astype(jnp.int32)
    cols = delta_cols[0].T
    tiles = delta_tiles[0]

    def rows_to(pick):
        return [(2 * x + c, pick(x, c)) for x in range(pairs) for c in range(2)]

    swap = rows_to(lambda x, c: 2 * x + 1 - c)

    def back(dx):
        return rows_to(lambda x, c: 2 * ((x - dx) % pairs) + c)

    def ahead(dx, cross):
        return rows_to(lambda x, c: 2 * ((x + dx) % pairs) + (1 - c if cross else c))

    def permute(v, perm):
        return lax.ppermute(v, "rows", perm)

    stay = lambda v: pltpu.with_memory_space_constraint(v, pltpu.HBM)
    own = hidden_of(stay(gate_in), stay(up_in), stay(tenant_of_row.reshape(1, count)))
    away = [permute(own, back(dx)) for dx in range(1, pairs)]
    mate = permute(own, swap)
    d_self, d_mate, c_self, c_mate, tiles, weight, hot = near_of(
        cap, width, meta, cols, own, mate, stay(tiles), stay(down_weight)
    )
    d_near = permute(d_mate, swap)
    c_near = permute(c_mate, swap)
    away, c_self = lax.optimization_barrier((away, c_self))
    sent = []

    def send(message, perm):
        if len(sent) >= LAG:
            message, sent[-LAG] = lax.optimization_barrier((message, sent[-LAG]))
        sent.append(permute(message, perm))

    for dx in range(1, pairs):
        same = away[dx - 1]
        diag = permute(same, swap)
        mine, other, d_same, d_diag, both, far_hot = far_of(
            cap, groups, width, meta, cols, same, diag, tiles
        )
        other = permute(other, swap)
        for part, (start, sub) in enumerate(zip(starts, cuts)):
            from_w = weight if start else first_of(sub, both, weight)
            m_same, m_diag = send_of(
                cap, start, sub, far_hot, both, from_w, mine, other, d_same, d_diag
            )
            send(m_same, ahead(dx, False))
            send(m_diag, ahead(dx, True))
    out = []
    for part, (start, sub) in enumerate(zip(starts, cuts)):
        got = []
        for dx in range(1, pairs):
            first = 2 * ((dx - 1) * len(cuts) + part)
            got += sent[first : first + 2]
        terms = merge_of(
            cap, groups, nz, direct, bw, start, sub, meta, hot,
            d_self, d_near, c_self, c_near, *got,
        )
        if not direct:
            return lax.psum_scatter(terms[0], "tensor", scatter_dimension=1, tiled=True)
        total = terms[0]
        for dz in ORDER:
            perm = [(z, (z + dz) % nz) for z in range(nz)]
            total = total + lax.ppermute(terms[dz], "tensor", perm).astype(F32)
        out.append(total.astype(BF))
    return jnp.concatenate(out, axis=1)


def solution(mesh):
    groups, nz = mesh.shape["rows"], mesh.shape["tensor"]
    return jax.shard_map(
        functools.partial(shards, groups, nz),
        mesh=mesh,
        in_specs=(
            P(("replica", "rows"), "tensor"),
            P(("replica", "rows"), "tensor"),
            P("tensor", "rows"),
            P("rows", "tensor", None, None, None),
            P("rows", "tensor", None),
            P(("replica", "rows"), None),
        ),
        out_specs=P(("replica", "rows"), "tensor"),
        check_vma=False,
    )
```

```python
import functools

import jax
import jax.numpy as jnp
from jax import lax
from jax.experimental import pallas as pl
from jax.experimental.pallas import tpu as pltpu
from jax.sharding import PartitionSpec as P

BF = jnp.bfloat16
F32 = jnp.float32
LANES = 128
VMEM_LIMIT = 16 * 1024 * 1024
PARTS = (2, 3, 3)
LAG = 5
ORDER = (1, 2, 3)


def params():
    return pltpu.CompilerParams(vmem_limit_bytes=VMEM_LIMIT)


def whole():
    return pl.BlockSpec(memory_space=pltpu.VMEM)


def smem():
    return pl.BlockSpec(memory_space=pltpu.SMEM)


def hidden_kernel(chunks, tenant_hbm, gate_hbm, up_hbm, out_ref, tenant_ref, gate_ref, up_ref, sem):
    count, feats = gate_ref.shape
    rows = count // chunks
    copies = [pltpu.make_async_copy(tenant_hbm, tenant_ref, sem.at[2 * chunks])]
    for i in range(chunks):
        at = pl.ds(i * rows, rows)
        copies.append(pltpu.make_async_copy(gate_hbm.at[at], gate_ref.at[at], sem.at[2 * i]))
        copies.append(pltpu.make_async_copy(up_hbm.at[at], up_ref.at[at], sem.at[2 * i + 1]))
    for copy in copies:
        copy.start()
    copies[0].wait()
    row = jnp.broadcast_to(tenant_ref[...].astype(F32), (count, count))
    diagonal = lax.broadcasted_iota(jnp.int32, (count, count), 0) == lax.broadcasted_iota(
        jnp.int32, (count, count), 1
    )
    column = jnp.sum(jnp.where(diagonal, row, 0.0), axis=1, keepdims=True)
    out_ref[:, feats:] = jnp.broadcast_to(column, (count, LANES)).astype(BF)
    for i in range(chunks):
        copies[2 * i + 1].wait()
        copies[2 * i + 2].wait()
        at = pl.ds(i * rows, rows)
        for start in range(0, feats, 512):
            to = pl.ds(start, min(512, feats - start))
            v = gate_ref[at, to].astype(F32)
            out_ref[at, to] = (v / (1.0 + jnp.exp(-v)) * up_ref[at, to].astype(F32)).astype(BF)


def hidden_of(gate, up, tenant):
    count, feats = gate.shape
    chunks = 4 if count % 64 == 0 else 1
    return pl.pallas_call(
        functools.partial(hidden_kernel, chunks),
        out_shape=jax.ShapeDtypeStruct((count, feats + LANES), BF),
        in_specs=[pl.BlockSpec(memory_space=pltpu.HBM)] * 3,
        out_specs=whole(),
        scratch_shapes=[
            pltpu.VMEM((1, count), jnp.int32),
            pltpu.VMEM((count, feats), BF),
            pltpu.VMEM((count, feats), BF),
            pltpu.SemaphoreType.DMA((2 * chunks + 1,)),
        ],
        compiler_params=params(),
        name="hidden",
        cost_estimate=pl.CostEstimate(
            flops=6 * count * feats, bytes_accessed=6 * count * feats, transcendentals=count * feats
        ),
    )(tenant, gate, up)


def slots_of(tenants, tenant):
    count = tenants.shape[0]
    mine = tenants == tenant.astype(F32)
    ones = jnp.where(mine, 1.0, 0.0).astype(BF)
    above = lax.broadcasted_iota(jnp.int32, (count, count), 0) > lax.broadcasted_iota(
        jnp.int32, (count, count), 1
    )
    earlier = jnp.dot(jnp.where(above, 1.0, 0.0).astype(BF), ones, preferred_element_type=F32)
    return jnp.where(mine, earlier, -1024.0)


def one_hot(slots, offset):
    lanes = lax.broadcasted_iota(jnp.int32, slots.shape, 1).astype(F32)
    return jnp.where(slots + offset == lanes, 1.0, 0.0).astype(BF)


def tenant_lanes(hidden_ref):
    return hidden_ref[:, hidden_ref.shape[1] - LANES :].astype(F32)


def pack_rows(cap, me, a_ref, b_ref, packed):
    feats = packed.shape[1]
    hot = jnp.concatenate(
        [
            one_hot(slots_of(tenant_lanes(a_ref), me), 0),
            one_hot(slots_of(tenant_lanes(b_ref), me), cap),
        ],
        axis=0,
    )
    for start in range(0, feats, 512):
        at = pl.ds(start, min(512, feats - start))
        both = jnp.concatenate([a_ref[:, at], b_ref[:, at]], axis=0)
        rows = lax.dot_general(hot, both, (((0,), (0,)), ((), ())), preferred_element_type=F32)
        packed[:, at] = rows[: 2 * cap].astype(BF)


def add_tiles(first, last, cols_ref, packed, tiles_ref, acc):
    per_row = tiles_ref.shape[1]
    for row in range(first, last):
        lhs = packed[:, row * LANES : (row + 1) * LANES]
        rhs = jnp.concatenate([tiles_ref[row, j] for j in range(per_row)], axis=1)
        prods = jnp.dot(lhs, rhs, preferred_element_type=F32)
        at = [cols_ref[j, row] for j in range(per_row)]
        old = [acc[at[j]] for j in range(per_row)]
        for j in range(per_row):
            acc[at[j]] = old[j] + prods[:, j * LANES : (j + 1) * LANES]


def owner_hots(cap, pairs, me, own_ref, hot_ref):
    tenants = tenant_lanes(own_ref)
    mate = me + 1 - 2 * (me % 2)
    hot_ref[0] = one_hot(slots_of(tenants, me), 0) + one_hot(slots_of(tenants, mate), cap)
    away = 2 * (pairs - 1)
    for dx in range(1, pairs):
        source = lax.rem(me // 2 + pairs - dx, pairs)
        for k, owner in enumerate((2 * source + me % 2, 2 * source + 1 - me % 2)):
            slots = slots_of(tenants, owner)
            for block in range(away):
                hot_ref[1 + (2 * (dx - 1) + k) * away + block] = one_hot(slots, block * cap)


def near_kernel(cap, nt, nw, *refs):
    meta_ref, cols_ref, a_ref, b_ref, tiles_ref, w_ref = refs[:6]
    da_ref, db_ref, ca_ref, cb_ref, tv_ref, wv_ref, hot_ref = refs[6:13]
    packed, acc, both, tsem, wsem = refs[13:]
    count = a_ref.shape[0]
    feats, bw = w_ref.shape
    nblk = tiles_ref.shape[0]
    tpart, wpart = nblk // nt, bw // nw
    width_pairs = da_ref.shape[1] // (2 * bw)
    tcopies = [
        pltpu.make_async_copy(
            tiles_ref.at[pl.ds(i * tpart, tpart)], tv_ref.at[pl.ds(i * tpart, tpart)], tsem.at[i]
        )
        for i in range(nt)
    ]
    wcopies = [
        pltpu.make_async_copy(
            w_ref.at[:, pl.ds(i * wpart, wpart)], wv_ref.at[:, pl.ds(i * wpart, wpart)], wsem.at[i]
        )
        for i in range(nw)
    ]
    for copy in tcopies + wcopies:
        copy.start()
    pack_rows(cap, meta_ref[0], a_ref, b_ref, packed)
    acc[...] = jnp.zeros_like(acc)
    both[:count] = a_ref[:, :feats]
    both[count:] = b_ref[:, :feats]
    owner_hots(cap, width_pairs, meta_ref[0], a_ref, hot_ref)
    for i in range(nt):
        tcopies[i].wait()
        add_tiles(i * tpart, (i + 1) * tpart, cols_ref, packed, tv_ref, acc)
    for n in range(acc.shape[0]):
        got = acc[n]
        da_ref[:, n * LANES : (n + 1) * LANES] = got[:cap].astype(BF)
        db_ref[:, n * LANES : (n + 1) * LANES] = got[cap:].astype(BF)
    for i in range(nw):
        at = slice(i * wpart, (i + 1) * wpart)
        wcopies[i].wait()
        total = jnp.dot(both[...], wv_ref[:, at], preferred_element_type=F32)
        ca_ref[:, at] = total[:count].astype(BF)
        cb_ref[:, at] = total[count:].astype(BF)


def near_of(cap, width, meta, cols, a, b, tiles, weight):
    count = a.shape[0]
    feats, bw = weight.shape
    nblk = tiles.shape[0]
    nt, nw = (4 if nblk % 4 == 0 else 1), max(1, bw // 512)
    hots = 1 + (width // bw - 2) ** 2
    any_space = pl.BlockSpec(memory_space=pltpu.HBM)
    return pl.pallas_call(
        functools.partial(near_kernel, cap, nt, nw),
        in_specs=[smem(), smem(), whole(), whole(), any_space, any_space],
        out_specs=[whole()] * 7,
        out_shape=[
            jax.ShapeDtypeStruct((cap, width), BF),
            jax.ShapeDtypeStruct((cap, width), BF),
            jax.ShapeDtypeStruct((count, bw), BF),
            jax.ShapeDtypeStruct((count, bw), BF),
            pltpu.VMEM(tiles.shape, BF),
            pltpu.VMEM(weight.shape, BF),
            jax.ShapeDtypeStruct((hots, count, LANES), BF),
        ],
        scratch_shapes=[
            pltpu.VMEM((2 * cap, feats), BF),
            pltpu.VMEM((width // LANES, 2 * cap, LANES), F32),
            pltpu.VMEM((2 * count, feats), BF),
            pltpu.SemaphoreType.DMA((nt,)),
            pltpu.SemaphoreType.DMA((nw,)),
        ],
        compiler_params=params(),
        name="near",
        cost_estimate=pl.CostEstimate(
            flops=4 * count * feats * bw,
            bytes_accessed=4 * weight.size + 4 * tiles.size,
            transcendentals=0,
        ),
    )(meta, cols, a, b, tiles, weight)


def far_kernel(cap, bw, *refs):
    meta_ref, cols_ref, a_ref, b_ref, tiles_ref, own_ref, mate_ref, da_ref, db_ref, both_ref, hot_ref, packed, acc = refs
    count, feats = a_ref.shape[0], packed.shape[1]
    both_ref[:count] = a_ref[:, :feats]
    both_ref[count:] = b_ref[:, :feats]
    me = meta_ref[0]
    chip = me // 2
    ncol = acc.shape[0]
    tiles = bw // LANES
    pairs = ncol // (2 * tiles)
    mate = me + 1 - 2 * (me % 2)
    for g, ref in enumerate((a_ref, b_ref)):
        tenants = tenant_lanes(ref)
        hot_ref[g * count : (g + 1) * count] = one_hot(slots_of(tenants, me), g * cap) + one_hot(
            slots_of(tenants, mate), (3 - g) * cap
        )
    pack_rows(cap, me, a_ref, b_ref, packed)
    acc[...] = jnp.zeros_like(acc)
    add_tiles(0, tiles_ref.shape[0], cols_ref, packed, tiles_ref, acc)
    for n in range(tiles):
        at = slice(n * LANES, (n + 1) * LANES)
        mate_ref[:, at] = acc[(me + 1 - 2 * (me % 2)) * tiles + n].astype(BF)
        own_ref[:, at] = acc[me * tiles + n].astype(BF)
        got = []
        for e in range(1, pairs):
            first = lax.rem(chip + e, pairs) * 2 * tiles
            got += [acc[first + n], acc[first + tiles + n]]
        da_ref[:, at] = jnp.concatenate([v[:cap] for v in got], axis=0).astype(BF)
        db_ref[:, at] = jnp.concatenate([v[cap:] for v in got], axis=0).astype(BF)


def far_of(cap, groups, width, meta, cols, a, b, tiles):
    feats = tiles.shape[0] * LANES
    bw = width // groups
    away = (groups - 2) * cap
    return pl.pallas_call(
        functools.partial(far_kernel, cap, bw),
        in_specs=[smem(), smem(), whole(), whole(), whole()],
        out_specs=[whole()] * 6,
        out_shape=[jax.ShapeDtypeStruct((rows, bw), BF) for rows in (2 * cap, 2 * cap, away, away)]
        + [jax.ShapeDtypeStruct((2 * a.shape[0], n), BF) for n in (feats, LANES)],
        scratch_shapes=[
            pltpu.VMEM((2 * cap, feats), BF),
            pltpu.VMEM((width // LANES, 2 * cap, LANES), F32),
        ],
        compiler_params=params(),
        name="far",
        cost_estimate=pl.CostEstimate(
            flops=16 * cap * tiles.size, bytes_accessed=2 * tiles.size, transcendentals=0
        ),
    )(meta, cols, a, b, tiles)


def first_kernel(both, w_ref, out_ref):
    sub = out_ref.shape[1]
    step = 256 if sub % 256 == 0 else LANES
    for n in range(0, sub, step):
        at = pl.ds(n, step)
        out_ref[:, at] = jnp.dot(both[...], w_ref[:, at], preferred_element_type=F32)


def first_of(sub, both, weight):
    return pl.pallas_call(
        first_kernel,
        in_specs=[whole()] * 2,
        out_specs=whole(),
        out_shape=jax.ShapeDtypeStruct((both.shape[0], sub), F32),
        compiler_params=params(),
        name="first",
        cost_estimate=pl.CostEstimate(
            flops=2 * both.size * sub, bytes_accessed=2 * weight.shape[0] * sub, transcendentals=0
        ),
    )(both, weight)


def send_kernel(cap, start, *refs):
    hot_ref, both, w_ref, mine_ref, other_ref, da_ref, db_ref, ma_ref, mb_ref = refs
    count = both.shape[0] // 2
    sub = ma_ref.shape[1]
    hot = hot_ref[:, : 4 * cap]
    step = 256 if sub % 256 == 0 else LANES
    for n in range(0, sub, step):
        at, to = pl.ds(start + n, step), pl.ds(n, step)
        if start == 0:
            total = w_ref[:, to]
        else:
            total = jnp.dot(both[...], w_ref[:, at], preferred_element_type=F32)
        rows = jnp.concatenate([mine_ref[:, at], other_ref[:, at]], axis=0)
        total += jnp.dot(hot, rows, preferred_element_type=F32)
        ma_ref[:count, to] = total[:count].astype(BF)
        mb_ref[:count, to] = total[count:].astype(BF)
    ma_ref[count:] = da_ref[:, pl.ds(start, sub)]
    mb_ref[count:] = db_ref[:, pl.ds(start, sub)]


def send_of(cap, start, sub, hot, both, weight, mine, other, da, db):
    count = both.shape[0] // 2
    feats = both.shape[1]
    rows = count + da.shape[0]
    return pl.pallas_call(
        functools.partial(send_kernel, cap, start),
        in_specs=[whole()] * 7,
        out_specs=[whole()] * 2,
        out_shape=[jax.ShapeDtypeStruct((rows, sub), BF)] * 2,
        compiler_params=params(),
        name="send",
        cost_estimate=pl.CostEstimate(
            flops=4 * count * feats * sub, bytes_accessed=2 * feats * sub, transcendentals=0
        ),
    )(hot, both, weight, mine, other, da, db)


def merge_kernel(cap, groups, nz, bw, start, *refs):
    meta_ref, hot_ref, dself_ref, dmate_ref, cself_ref, cmate_ref = refs[:6]
    pairs = groups // 2
    far = refs[6 : 6 + 2 * (pairs - 1)]
    outs, acc = refs[6 + 2 * (pairs - 1) : -1], refs[-1]
    sub = acc.shape[2]
    me, z = meta_ref[0], meta_ref[1]
    mate = me + 1 - 2 * (me % 2)
    chip = me // 2
    count = acc.shape[1]
    near = hot_ref[0][:, : 2 * cap]
    for block in range(groups):
        at = pl.ds(block * bw + start, sub)
        rows = jnp.concatenate([dself_ref[:, at].astype(F32), dmate_ref[:, at].astype(F32)], axis=0)
        acc[block] = jnp.dot(near, rows.astype(BF), preferred_element_type=F32)
    acc[me] += cself_ref[:, start : start + sub].astype(F32)
    acc[mate] += cmate_ref[:, start : start + sub].astype(F32)
    away = groups - 2
    for dx in range(1, pairs):
        source = lax.rem(chip + pairs - dx, pairs)
        for k, owner in enumerate((2 * source + me % 2, 2 * source + 1 - me % 2)):
            got = far[2 * (dx - 1) + k]
            acc[owner] += got[:count].astype(F32)
            delta = got[count:]
            for e in range(1, pairs):
                target = lax.rem(source + e, pairs)
                for half in range(2):
                    block = 2 * (e - 1) + half
                    hot = hot_ref[1 + (2 * (dx - 1) + k) * away + block][:, : delta.shape[0]]
                    acc[2 * target + half] += jnp.dot(hot, delta, preferred_element_type=F32)
    if len(outs) == nz:
        for dz in range(nz):
            outs[dz][...] = acc[lax.rem(z + dz, nz)].astype(outs[dz].dtype)
    else:
        for block in range(groups):
            outs[0][:, block * bw : (block + 1) * bw] = acc[block].astype(BF)


def merge_of(cap, groups, nz, direct, bw, start, sub, meta, hot, *pieces):
    count = hot.shape[1]
    if direct:
        shapes = [jax.ShapeDtypeStruct((count, sub), F32 if dz == 0 else BF) for dz in range(nz)]
    else:
        shapes = [jax.ShapeDtypeStruct((count, groups * bw), BF)]
    return pl.pallas_call(
        functools.partial(merge_kernel, cap, groups, nz, bw, start),
        out_shape=shapes,
        in_specs=[smem()] + [whole()] * (1 + len(pieces)),
        out_specs=[whole()] * len(shapes),
        scratch_shapes=[pltpu.VMEM((groups, count, sub), F32)],
        compiler_params=params(),
        name="merge",
        cost_estimate=pl.CostEstimate(
            flops=4 * count * groups * sub * LANES, bytes_accessed=8 * count * groups * sub, transcendentals=0
        ),
    )(meta, hot, *pieces)


def shards(groups, nz, gate_in, up_in, down_weight, delta_tiles, delta_cols, tenant_of_row):
    count = gate_in.shape[0]
    pairs = groups // 2
    bw = down_weight.shape[1]
    width = bw * groups
    cap = -(-(count * 3 // (2 * groups)) // 8) * 8
    direct = nz == groups == 4 and bw % (LANES * sum(PARTS)) == 0
    cuts = [bw * p // sum(PARTS) for p in PARTS] if direct else [bw]
    starts = [sum(cuts[:i]) for i in range(len(cuts))]
    meta = jnp.stack([lax.axis_index("rows"), lax.axis_index("tensor")]).astype(jnp.int32)
    cols = delta_cols[0].T
    tiles = delta_tiles[0]

    def rows_to(pick):
        return [(2 * x + c, pick(x, c)) for x in range(pairs) for c in range(2)]

    swap = rows_to(lambda x, c: 2 * x + 1 - c)

    def back(dx):
        return rows_to(lambda x, c: 2 * ((x - dx) % pairs) + c)

    def ahead(dx, cross):
        return rows_to(lambda x, c: 2 * ((x + dx) % pairs) + (1 - c if cross else c))

    def permute(v, perm):
        return lax.ppermute(v, "rows", perm)

    stay = lambda v: pltpu.with_memory_space_constraint(v, pltpu.HBM)
    own = hidden_of(stay(gate_in), stay(up_in), stay(tenant_of_row.reshape(1, count)))
    away = [permute(own, back(dx)) for dx in range(1, pairs)]
    mate = permute(own, swap)
    d_self, d_mate, c_self, c_mate, tiles, weight, hot = near_of(
        cap, width, meta, cols, own, mate, stay(tiles), stay(down_weight)
    )
    d_near = permute(d_mate, swap)
    c_near = permute(c_mate, swap)
    away, c_self = lax.optimization_barrier((away, c_self))
    sent = []

    def send(message, perm):
        if len(sent) >= LAG:
            message, sent[-LAG] = lax.optimization_barrier((message, sent[-LAG]))
        sent.append(permute(message, perm))

    for dx in range(1, pairs):
        same = away[dx - 1]
        diag = permute(same, swap)
        mine, other, d_same, d_diag, both, far_hot = far_of(
            cap, groups, width, meta, cols, same, diag, tiles
        )
        other = permute(other, swap)
        for part, (start, sub) in enumerate(zip(starts, cuts)):
            from_w = weight if start else first_of(sub, both, weight)
            m_same, m_diag = send_of(
                cap, start, sub, far_hot, both, from_w, mine, other, d_same, d_diag
            )
            send(m_same, ahead(dx, False))
            send(m_diag, ahead(dx, True))
    out = []
    for part, (start, sub) in enumerate(zip(starts, cuts)):
        got = []
        for dx in range(1, pairs):
            first = 2 * ((dx - 1) * len(cuts) + part)
            got += sent[first : first + 2]
        terms = merge_of(
            cap, groups, nz, direct, bw, start, sub, meta, hot,
            d_self, d_near, c_self, c_near, *got,
        )
        if not direct:
            return lax.psum_scatter(terms[0], "tensor", scatter_dimension=1, tiled=True)
        total = terms[0]
        for dz in ORDER:
            perm = [(z, (z + dz) % nz) for z in range(nz)]
            total = total + lax.ppermute(terms[dz], "tensor", perm).astype(F32)
        out.append(total.astype(BF))
    return jnp.concatenate(out, axis=1)


def solution(mesh):
    groups, nz = mesh.shape["rows"], mesh.shape["tensor"]
    return jax.shard_map(
        functools.partial(shards, groups, nz),
        mesh=mesh,
        in_specs=(
            P(("replica", "rows"), "tensor"),
            P(("replica", "rows"), "tensor"),
            P("tensor", "rows"),
            P("rows", "tensor", None, None, None),
            P("rows", "tensor", None),
            P(("replica", "rows"), None),
        ),
        out_specs=P(("replica", "rows"), "tensor"),
        check_vma=False,
    )
```
